512 devices in a mesh: kg: 16 (over z_hi, y, core), pt: 32 (over x, z_lo).
Axes of the slice: x: 4, y: 4, z: 16 (z_hi: 2, z_lo: 8; z = z_hi * 8 + z_lo), core: 2. Of those that a mesh axis runs over, the one named last changes fastest.
Arguments:
- left_orbitals: bfloat16 [2, 64, 4096, 512], P(None, 'kg', 'pt'), may hold values from -6 to 6
- right_orbitals: bfloat16 [2, 64, 512, 512], P(None, 'kg', 'pt'), may hold values from -0.25 to 0.25
- coulomb: bfloat16 [64, 512, 4096], P(None, 'kg', 'pt'), may hold values from 0.049804688 to 0.5
Outputs:
- exchange_applied: float32 [2, 64, 4096, 512], P(None, 'kg', 'pt')
The draws below stay inside these ranges and needn't reach their ends.
All inputs are finite; a program needn't handle non-finite values.
Results may differ from the reference program's by a relative error of at most 0.0038.
Values may be sent and summed in bfloat16 or wider, within the bound.
No kernel may reach another device: no remote copies, remote signals or barrier semaphores. Data moves between devices by JAX's collectives and lax.ppermute only.
A program may use at most 64 MiB of HBM per device.

```python
import math
import jax
import jax.numpy as jnp
from jax import lax

NK = 64
NOCC = 512
NU = 512
MU = 4096


def level_of(key, extent, shards, low, high):
    level, own = 1.0, jax.random.fold_in(key, 6)
    for dim, shards_of in shards:
        heights = jnp.exp(jax.random.uniform(jax.random.fold_in(own, dim), (shards_of,), jnp.float32, low / len(shards), high / len(shards)))
        level = level * jnp.repeat(heights, extent[dim] // shards_of).reshape([-1 if axis == dim else 1 for axis in range(len(extent))])
    return level


def normal_values(key, extent, spread, most, cuts=(), held_as=jnp.bfloat16):
    drawn = jax.random.normal(key, extent, jnp.float32) * spread
    if len(cuts) > 0:
        drawn = level_of(key, extent, cuts, -0.22, 0.18) * drawn
    return jnp.clip(drawn, min=-most, max=most).astype(held_as)


def setup_inputs(seed: int = 0) -> dict:
    seeds = jax.random.split(jax.random.key(seed), 4)
    return {
        "left_orbitals": normal_values(seeds[0], (2, NK, MU, NOCC), 1.0, 6.0, ((1, 16), (2, 32))),
        "right_orbitals": normal_values(seeds[1], (2, NK, NU, NOCC), NOCC ** -0.5, 0.25, ((1, 16), (2, 32))),
        "coulomb": jnp.clip(jnp.exp(math.log(0.5) - 2.306499 * jax.random.uniform(seeds[2], (NK, NU, MU), jnp.float32) ** level_of(seeds[2], (NK, NU, MU), ((1, 16), (2, 32)), -0.2, 0.2)), 0.049804688, 0.5).astype(jnp.bfloat16),
    }


def dft_tables(count):
    index = jnp.arange(count, dtype=jnp.int32)
    digit_one = index // 16
    digit_two = (index // 4) % 4
    digit_three = index % 4
    phase = (digit_one[:, None] * digit_one[None, :] + digit_two[:, None] * digit_two[None, :] + digit_three[:, None] * digit_three[None, :]) % 4
    cos_table = jnp.where(phase == 0, 1.0, jnp.where(phase == 2, -1.0, 0.0)).astype(jnp.float32)
    sin_table = jnp.where(phase == 1, 1.0, jnp.where(phase == 3, -1.0, 0.0)).astype(jnp.float32)
    return cos_table, sin_table


def reference(left_orbitals, right_orbitals, coulomb):
    block_rows = min(256, MU)
    blocks = MU // block_rows
    cos_table, sin_table = dft_tables(NK)
    forward = jnp.concatenate([jnp.concatenate([cos_table, sin_table], 1), jnp.concatenate([-sin_table, cos_table], 1)], 0)
    backward = jnp.concatenate([jnp.concatenate([cos_table, -sin_table], 1), jnp.concatenate([sin_table, cos_table], 1)], 0)
    right_re = right_orbitals[0].astype(jnp.float32)
    right_im = right_orbitals[1].astype(jnp.float32)

    def one_block(number):
        start = (number * block_rows).astype(jnp.int32)
        left = lax.dynamic_slice_in_dim(left_orbitals, start, block_rows, 2).astype(jnp.float32)
        weights = lax.dynamic_slice_in_dim(coulomb, start, block_rows, 2).astype(jnp.float32)
        left_re, left_im = left[0], left[1]

        def cross(first, second):
            return jnp.einsum('kni,kmi->knm', first, second)

        pair_re = cross(right_re, left_re) + cross(right_im, left_im)
        pair_im = cross(right_re, left_im) - cross(right_im, left_re)
        pairs = jnp.stack([pair_re, pair_im]).astype(jnp.bfloat16).astype(jnp.float32)
        flat = pairs.reshape(2 * NK, -1)
        freq = jnp.dot(forward, flat, precision=lax.Precision.HIGHEST).reshape(pairs.shape)
        weighted = (weights[None] * freq).astype(jnp.bfloat16).astype(jnp.float32)
        spatial = jnp.dot(backward, weighted.reshape(2 * NK, -1), precision=lax.Precision.HIGHEST) * (1.0 / NK)
        kernel = spatial.astype(jnp.bfloat16).astype(jnp.float32).reshape(pairs.shape)

        def apply(first, second):
            return jnp.einsum('knm,kni->kmi', first, second)

        out_re = apply(kernel[0], right_re) - apply(kernel[1], right_im)
        out_im = apply(kernel[0], right_im) + apply(kernel[1], right_re)
        return jnp.stack([out_re, out_im])

    result = lax.map(one_block, jnp.arange(blocks, dtype=jnp.int32))
    result = jnp.moveaxis(result, 0, 2)
    return result.reshape(2, NK, MU, NOCC)
```

```python
import jax
import jax.numpy as jnp
from jax import lax
from jax.experimental import pallas as pl
from jax.experimental.pallas import tpu as pltpu
from jax.sharding import PartitionSpec as P

XS, ZS = 4, 8
KG = 16
KL = 4
VMEM = pltpu.CompilerParams(vmem_limit_bytes=48 << 20)
Z_GROUPS = [[x * ZS + z for z in range(ZS)] for x in range(XS)]
X_GROUPS = [[x * ZS + z for x in range(XS)] for z in range(ZS)]


def pairs_kernel(left_ref, right_ref, out_ref):
    a_re, a_im = left_ref[0, 0], left_ref[1, 0]
    mu, orbitals = a_re.shape
    b_re = right_ref[:, 0, 0].reshape(-1, orbitals)
    b_im = right_ref[:, 1, 0].reshape(-1, orbitals)
    nt = (((1,), (1,)), ((), ()))
    first = jnp.concatenate([a_re, a_im], 0)
    second = jnp.concatenate([a_im, -a_re], 0)
    both = lax.dot_general(b_re, first, nt, preferred_element_type=jnp.float32) + lax.dot_general(
        b_im, second, nt, preferred_element_type=jnp.float32
    )
    both = both.astype(jnp.bfloat16)
    shape = (out_ref.shape[0], out_ref.shape[3], mu)
    out_ref[:, 0, 0] = both[:, :mu].reshape(shape)
    out_ref[:, 1, 0] = both[:, mu:].reshape(shape)


def make_pairs(left, right):
    pts, _, kl, nus, orbitals = right.shape
    mu = left.shape[2]
    rows = pts * nus // KG
    return pl.pallas_call(
        pairs_kernel,
        grid=(kl,),
        in_specs=[
            pl.BlockSpec((2, 1, mu, orbitals), lambda k: (0, k, 0, 0)),
            pl.BlockSpec((pts, 2, 1, nus, orbitals), lambda k: (0, 0, k, 0, 0)),
        ],
        out_specs=pl.BlockSpec((KG, 2, 1, rows, mu), lambda k: (0, 0, k, 0, 0)),
        out_shape=jax.ShapeDtypeStruct((KG, 2, kl, rows, mu), jnp.bfloat16),
        compiler_params=VMEM,
        cost_estimate=pl.CostEstimate(
            flops=8 * kl * pts * nus * mu * orbitals, bytes_accessed=6 << 20, transcendentals=0
        ),
        name="pairs",
    )(left, right)


def dft4(values, sign):
    (r0, i0), (r1, i1), (r2, i2), (r3, i3) = values
    ar, ai, br, bi = r0 + r2, i0 + i2, r0 - r2, i0 - i2
    cr, ci, dr, di = r1 + r3, i1 + i3, r1 - r3, i1 - i3
    if sign < 0:
        return [(ar + cr, ai + ci), (br + di, bi - dr), (ar - cr, ai - ci), (br - di, bi + dr)]
    return [(ar + cr, ai + ci), (br - di, bi + dr), (ar - cr, ai - ci), (br + di, bi - dr)]


def dft16(values, sign):
    out = list(values)
    for slow in range(4):
        out[4 * slow : 4 * slow + 4] = dft4(out[4 * slow : 4 * slow + 4], sign)
    for fast in range(4):
        out[fast::4] = dft4(out[fast::4], sign)
    return out


def spectral_kernel(x_ref, c_ref, out_ref, work_ref):
    rows = work_ref.shape[2]
    for top in range(4):
        values = []
        for low in range(16):
            kg, kl = 4 * top + low // 4, low % 4
            values.append(tuple(x_ref[kg, part, kl].astype(jnp.float32) for part in range(2)))
        for low, (re, im) in enumerate(dft16(values, -1)):
            work_ref[0, 16 * top + low] = re
            work_ref[1, 16 * top + low] = im
    for low in range(16):
        values = [(work_ref[0, 16 * top + low], work_ref[1, 16 * top + low]) for top in range(4)]
        freq = dft4(values, -1)
        weighted = []
        for top, (re, im) in enumerate(freq):
            c = c_ref[16 * top + low].astype(jnp.float32)
            weighted.append(tuple((c * part).astype(jnp.bfloat16).astype(jnp.float32) for part in (re, im)))
        for top, (re, im) in enumerate(dft4(weighted, 1)):
            work_ref[0, 16 * top + low] = re
            work_ref[1, 16 * top + low] = im
    for top in range(4):
        values = [(work_ref[0, 16 * top + low], work_ref[1, 16 * top + low]) for low in range(16)]
        for low, parts in enumerate(dft16(values, 1)):
            kg, kl = 4 * top + low // 4, low % 4
            for part in range(2):
                out_ref[kg, part, kl] = (parts[part] * (1.0 / 64.0)).astype(jnp.bfloat16)


def spectral(x, coulomb):
    kg, _, kl, nus, mu = x.shape
    rows = 16
    return pl.pallas_call(
        spectral_kernel,
        grid=(nus // rows,),
        in_specs=[
            pl.BlockSpec((kg, 2, kl, rows, mu), lambda n: (0, 0, 0, n, 0)),
            pl.BlockSpec((kg * kl, rows, mu), lambda n: (0, n, 0)),
        ],
        out_specs=pl.BlockSpec((kg, 2, kl, rows, mu), lambda n: (0, 0, 0, n, 0)),
        out_shape=jax.ShapeDtypeStruct(x.shape, jnp.bfloat16),
        scratch_shapes=[pltpu.VMEM((2, kg * kl, rows, mu), jnp.float32)],
        compiler_params=VMEM,
        cost_estimate=pl.CostEstimate(flops=32 * kg * kl * nus * mu, bytes_accessed=5 << 19, transcendentals=0),
        name="spectral",
    )(x, coulomb)


def apply_kernel(kernel_ref, right_ref, out_ref):
    mu = kernel_ref.shape[4]
    orbitals = right_ref.shape[4]
    k_re = kernel_ref[:, 0, 0].reshape(-1, mu)
    k_im = kernel_ref[:, 1, 0].reshape(-1, mu)
    b_re = right_ref[:, 0, 0].reshape(-1, orbitals)
    b_im = right_ref[:, 1, 0].reshape(-1, orbitals)
    tn = (((0,), (0,)), ((), ()))
    first = jnp.concatenate([k_re, k_im], 1)
    second = jnp.concatenate([-k_im, k_re], 1)
    both = lax.dot_general(first, b_re, tn, preferred_element_type=jnp.float32) + lax.dot_general(
        second, b_im, tn, preferred_element_type=jnp.float32
    )
    out_ref[0, 0] = both[:mu]
    out_ref[1, 0] = both[mu:]


def apply(kernel, right):
    kg, _, kl, rows, mu = kernel.shape
    pts, _, _, nus, orbitals = right.shape
    return pl.pallas_call(
        apply_kernel,
        grid=(kl,),
        in_specs=[
            pl.BlockSpec((kg, 2, 1, rows, mu), lambda k: (0, 0, k, 0, 0)),
            pl.BlockSpec((pts, 2, 1, nus, orbitals), lambda k: (0, 0, k, 0, 0)),
        ],
        out_specs=pl.BlockSpec((2, 1, mu, orbitals), lambda k: (0, k, 0, 0)),
        out_shape=jax.ShapeDtypeStruct((2, kl, mu, orbitals), jnp.float32),
        compiler_params=VMEM,
        cost_estimate=pl.CostEstimate(
            flops=8 * kl * pts * nus * mu * orbitals, bytes_accessed=7 << 20, transcendentals=0
        ),
        name="apply",
    )(kernel, right)


def spread(block, groups):
    count = len(groups[0])
    stacked = jnp.broadcast_to(block[None], (count, *block.shape))
    return lax.all_to_all(stacked, "pt", split_axis=0, concat_axis=0, tiled=True, axis_index_groups=groups)


def on_device(left, right, coulomb):
    column = spread(right, Z_GROUPS)
    whole = spread(column, X_GROUPS).reshape(XS * ZS, *right.shape)
    pairs = make_pairs(left, whole)
    columns = lax.all_to_all(pairs, "kg", split_axis=0, concat_axis=0, tiled=True)
    spatial = spectral(columns, coulomb)
    kernel = lax.all_to_all(spatial, "kg", split_axis=0, concat_axis=0, tiled=True)
    return apply(kernel, whole)


def solution(mesh):
    in_specs = (P(None, "kg", "pt", None), P(None, "kg", "pt", None), P(None, "kg", "pt"))
    out_specs = P(None, "kg", "pt", None)
    return jax.shard_map(on_device, mesh=mesh, in_specs=in_specs, out_specs=out_specs, check_vma=False)
```

```python
import functools

import jax
import jax.numpy as jnp
from jax import lax
from jax.experimental import pallas as pl
from jax.experimental.pallas import tpu as pltpu
from jax.sharding import Mesh, PartitionSpec as P

XS, ZH, ZQ = 4, 2, 4
KG, KL = 16, 4
VMEM = pltpu.CompilerParams(vmem_limit_bytes=48 << 20)


def pairs_kernel(zh_ref, left_ref, right_ref, out_ref):
    a_re, a_im = left_ref[0, 0], left_ref[0, 1]
    mu, orbitals = a_re.shape
    nt = (((1,), (1,)), ((), ()))
    first = jnp.concatenate([a_re, a_im], 0)
    second = jnp.concatenate([a_im, -a_re], 0)
    for side in range(2):
        b_re = right_ref[:, :, 0, side].reshape(-1, orbitals)
        b_im = right_ref[:, :, 1, side].reshape(-1, orbitals)
        both = lax.dot_general(b_re, first, nt, preferred_element_type=jnp.float32) + lax.dot_general(
            b_im, second, nt, preferred_element_type=jnp.float32
        )
        both = both.astype(jnp.bfloat16)
        at = zh_ref[0] if side == 0 else 1 - zh_ref[0]
        shape = (XS, ZQ // 2, out_ref.shape[5], mu)
        out_ref[:, at, :, 0, 0] = both[:, :mu].reshape(shape)
        out_ref[:, at, :, 0, 1] = both[:, mu:].reshape(shape)


def make_pairs(zh, left, right):
    blocks, _, mu, orbitals = left.shape
    nus = right.shape[4]
    whole = pl.BlockSpec(right.shape, lambda m, zh: (0,) * 6)
    return pl.pallas_call(
        pairs_kernel,
        grid_spec=pltpu.PrefetchScalarGridSpec(
            num_scalar_prefetch=1,
            grid=(blocks,),
            in_specs=[pl.BlockSpec((1, 2, mu, orbitals), lambda m, zh: (m, 0, 0, 0)), whole],
            out_specs=pl.BlockSpec((XS, ZH, ZQ // 2, 1, 2, 2 * nus, mu), lambda m, zh: (0, 0, 0, m, 0, 0, 0)),
        ),
        out_shape=jax.ShapeDtypeStruct((XS, ZH, ZQ // 2, blocks, 2, 2 * nus, mu), jnp.bfloat16),
        compiler_params=VMEM,
        cost_estimate=pl.CostEstimate(
            flops=8 * blocks * 32 * nus * mu * orbitals, bytes_accessed=3 << 20, transcendentals=0
        ),
        name="pairs",
    )(zh, left, right)


def dft4(values, sign):
    (r0, i0), (r1, i1), (r2, i2), (r3, i3) = values
    ar, ai, br, bi = r0 + r2, i0 + i2, r0 - r2, i0 - i2
    cr, ci, dr, di = r1 + r3, i1 + i3, r1 - r3, i1 - i3
    if sign < 0:
        return [(ar + cr, ai + ci), (br + di, bi - dr), (ar - cr, ai - ci), (br - di, bi + dr)]
    return [(ar + cr, ai + ci), (br - di, bi + dr), (ar - cr, ai - ci), (br + di, bi - dr)]


def dft16(values, sign):
    out = list(values)
    for slow in range(4):
        out[4 * slow : 4 * slow + 4] = dft4(out[4 * slow : 4 * slow + 4], sign)
    for fast in range(4):
        out[fast::4] = dft4(out[fast::4], sign)
    return out


def spectral_kernel(x_ref, c_ref, out_ref, work_ref):
    for top in range(4):
        values = [
            tuple(x_ref[16 * top + low, part].astype(jnp.float32) for part in range(2)) for low in range(16)
        ]
        for low, (re, im) in enumerate(dft16(values, -1)):
            work_ref[0, 16 * top + low] = re
            work_ref[1, 16 * top + low] = im
    for low in range(16):
        values = [(work_ref[0, 16 * top + low], work_ref[1, 16 * top + low]) for top in range(4)]
        weighted = []
        for top, (re, im) in enumerate(dft4(values, -1)):
            c = c_ref[16 * top + low].astype(jnp.float32)
            weighted.append(tuple((c * part).astype(jnp.bfloat16).astype(jnp.float32) for part in (re, im)))
        for top, (re, im) in enumerate(dft4(weighted, 1)):
            work_ref[0, 16 * top + low] = re
            work_ref[1, 16 * top + low] = im
    for top in range(4):
        values = [(work_ref[0, 16 * top + low], work_ref[1, 16 * top + low]) for low in range(16)]
        for low, parts in enumerate(dft16(values, 1)):
            for part in range(2):
                out_ref[16 * top + low, part] = (parts[part] * (1.0 / 64.0)).astype(jnp.bfloat16)


def spectral(x, coulomb):
    count, _, nus, mu = x.shape
    rows = 16
    block = pl.BlockSpec((count, 2, rows, mu), lambda n: (0, 0, n, 0))
    return pl.pallas_call(
        spectral_kernel,
        grid=(nus // rows,),
        in_specs=[block, pl.BlockSpec((count, rows, mu), lambda n: (0, n, 0))],
        out_specs=block,
        out_shape=jax.ShapeDtypeStruct(x.shape, jnp.bfloat16),
        scratch_shapes=[pltpu.VMEM((2, count, rows, mu), jnp.float32)],
        compiler_params=VMEM,
        cost_estimate=pl.CostEstimate(flops=32 * count * nus * mu, bytes_accessed=5 << 19, transcendentals=0),
        name="spectral",
    )(x, coulomb)


def apply_kernel(zh_ref, kernel_ref, right_ref, out_ref):
    mu, orbitals = out_ref.shape[2:]
    tn = (((0,), (0,)), ((), ()))
    total = None
    for side in range(2):
        at = zh_ref[0] if side == 0 else 1 - zh_ref[0]
        k_re = kernel_ref[:, at, :, 0, 0].reshape(-1, mu)
        k_im = kernel_ref[:, at, :, 0, 1].reshape(-1, mu)
        b_re = right_ref[0, :, :, 0, side].reshape(-1, orbitals)
        b_im = right_ref[0, :, :, 1, side].reshape(-1, orbitals)
        first = jnp.concatenate([k_re, k_im], 1)
        second = jnp.concatenate([-k_im, k_re], 1)
        term = lax.dot_general(first, b_re, tn, preferred_element_type=jnp.float32) + lax.dot_general(
            second, b_im, tn, preferred_element_type=jnp.float32
        )
        total = term if total is None else total + term
    out_ref[0, 0] = total[:mu]
    out_ref[1, 0] = total[mu:]


def apply(zh, kernel, right):
    xs, zhs, pairs, kl, _, rows, mu = kernel.shape
    orbitals = right.shape[-1]
    return pl.pallas_call(
        apply_kernel,
        grid_spec=pltpu.PrefetchScalarGridSpec(
            num_scalar_prefetch=1,
            grid=(kl,),
            in_specs=[
                pl.BlockSpec((xs, zhs, pairs, 1, 2, rows, mu), lambda k, zh: (0, 0, 0, k, 0, 0, 0)),
                pl.BlockSpec((1, *right.shape[1:]), lambda k, zh: (k, 0, 0, 0, 0, 0, 0)),
            ],
            out_specs=pl.BlockSpec((2, 1, mu, orbitals), lambda k, zh: (0, k, 0, 0)),
        ),
        out_shape=jax.ShapeDtypeStruct((2, kl, mu, orbitals), jnp.float32),
        compiler_params=VMEM,
        cost_estimate=pl.CostEstimate(
            flops=8 * kl * xs * zhs * pairs * rows * mu * orbitals, bytes_accessed=7 << 20, transcendentals=0
        ),
        name="apply",
    )(zh, kernel, right)


def swap(blocks, axes):
    return lax.all_to_all(blocks, axes, split_axis=0, concat_axis=0, tiled=True)


def on_device(left, right, coulomb):
    parts, kl, nus, orbitals = right.shape
    mu = left.shape[2]
    zh = jnp.full((1,), lax.axis_index("zh"), jnp.int32)
    sides = jnp.stack([right, lax.ppermute(right, "zh", [(0, 1), (1, 0)])], 2)
    sides = jnp.broadcast_to(
        sides.transpose(1, 0, 2, 3, 4)[:, None], (kl, ZQ, parts, 2, nus, orbitals)
    )
    mine = swap(sides.reshape(kl * ZQ, parts, 2, nus, orbitals), ("x", "zq"))
    mine = mine.reshape(XS, ZQ, parts, 2, nus, orbitals)
    rows = swap(jnp.swapaxes(left, 0, 1), "x")
    pairs = make_pairs(zh, rows, mine)
    columns = swap(pairs.reshape(KG * XS, parts, 2 * nus, mu), ("kg", "x"))
    kernel = swap(spectral(columns, coulomb).reshape(KG, KL, parts, 2 * nus, mu), "kg")
    whole = lax.all_gather(mine, "x", axis=0)
    return apply(zh, kernel.reshape(XS, ZH, ZQ // 2, KL, parts, 2 * nus, mu), whole)


def solution(mesh):
    split = Mesh(mesh.devices.reshape(KG, XS, ZH, ZQ), ("kg", "x", "zh", "zq"))
    points = ("x", "zh", "zq")
    in_specs = (P(None, "kg", points, None), P(None, "kg", points, None), P(None, "kg", points))
    out_specs = P(None, "kg", points, None)
    return jax.shard_map(on_device, mesh=split, in_specs=in_specs, out_specs=out_specs, check_vma=False)
```

```python
import functools

import jax
import jax.numpy as jnp
from jax import lax
from jax.experimental import pallas as pl
from jax.experimental.pallas import tpu as pltpu
from jax.sharding import Mesh, PartitionSpec as P

XS, ZH, ZQ = 4, 2, 4
KG, KL = 16, 4
VMEM = pltpu.CompilerParams(vmem_limit_bytes=48 << 20)


def pairs_kernel(place_ref, *refs):
    lefts, right_ref, out_ref = refs[:XS], refs[XS], refs[-1]
    mu, orbitals = lefts[0].shape[2:]
    nt = (((1,), (1,)), ((), ()))
    b_re = right_ref[:, :, 0, 0].reshape(-1, orbitals)
    b_im = right_ref[:, :, 1, 0].reshape(-1, orbitals)
    shape = (XS, ZQ // 2, out_ref.shape[5], mu)
    for d, left_ref in enumerate(lefts):
        a_re, a_im = left_ref[0, 0], left_ref[1, 0]
        first = jnp.concatenate([a_re, a_im], 0)
        second = jnp.concatenate([a_im, -a_re], 0)
        both = lax.dot_general(b_re, first, nt, preferred_element_type=jnp.float32) + lax.dot_general(
            b_im, second, nt, preferred_element_type=jnp.float32
        )
        both = both.astype(jnp.bfloat16)
        at = (place_ref[1] + XS - d) % XS
        out_ref[:, 0, :, at, 0] = both[:, :mu].reshape(shape)
        out_ref[:, 0, :, at, 1] = both[:, mu:].reshape(shape)


def make_pairs(place, lefts, right):
    _, _, mu, orbitals = lefts[0].shape
    nus = right.shape[4]
    one = (2, 1, mu, orbitals)
    left_specs = [pl.BlockSpec(one, lambda side, place: (0, place[1], 0, 0))]
    left_specs += [pl.BlockSpec(one, lambda side, place: (0, 0, 0, 0))] * (XS - 1)
    return pl.pallas_call(
        pairs_kernel,
        grid_spec=pltpu.PrefetchScalarGridSpec(
            num_scalar_prefetch=1,
            grid=(2,),
            in_specs=left_specs
            + [pl.BlockSpec((XS, ZQ, 2, 1, nus, orbitals), lambda side, place: (0, 0, 0, side, 0, 0))],
            out_specs=pl.BlockSpec(
                (XS, 1, ZQ // 2, XS, 2, 2 * nus, mu), lambda side, place: (0, (place[0] + side) % ZH, 0, 0, 0, 0, 0)
            ),
        ),
        out_shape=jax.ShapeDtypeStruct((XS, ZH, ZQ // 2, XS, 2, 2 * nus, mu), jnp.bfloat16),
        compiler_params=VMEM,
        cost_estimate=pl.CostEstimate(
            flops=16 * XS * XS * ZQ * nus * mu * orbitals, bytes_accessed=3 << 20, transcendentals=0
        ),
        name="pairs",
    )(place, *lefts, right)


def dft4(values, sign):
    (r0, i0), (r1, i1), (r2, i2), (r3, i3) = values
    ar, ai, br, bi = r0 + r2, i0 + i2, r0 - r2, i0 - i2
    cr, ci, dr, di = r1 + r3, i1 + i3, r1 - r3, i1 - i3
    if sign < 0:
        return [(ar + cr, ai + ci), (br + di, bi - dr), (ar - cr, ai - ci), (br - di, bi + dr)]
    return [(ar + cr, ai + ci), (br - di, bi + dr), (ar - cr, ai - ci), (br + di, bi - dr)]


def dft16(values, sign):
    out = list(values)
    for slow in range(4):
        out[4 * slow : 4 * slow + 4] = dft4(out[4 * slow : 4 * slow + 4], sign)
    for fast in range(4):
        out[fast::4] = dft4(out[fast::4], sign)
    return out


def spectral_kernel(x_ref, c_ref, out_ref, work_ref):
    for top in range(4):
        values = [
            tuple(x_ref[16 * top + low, part].astype(jnp.float32) for part in range(2)) for low in range(16)
        ]
        for low, (re, im) in enumerate(dft16(values, -1)):
            work_ref[0, 16 * top + low] = re
            work_ref[1, 16 * top + low] = im
    for low in range(16):
        values = [(work_ref[0, 16 * top + low], work_ref[1, 16 * top + low]) for top in range(4)]
        weighted = []
        for top, (re, im) in enumerate(dft4(values, -1)):
            c = c_ref[16 * top + low].astype(jnp.float32)
            weighted.append(tuple((c * part).astype(jnp.bfloat16).astype(jnp.float32) for part in (re, im)))
        for top, (re, im) in enumerate(dft4(weighted, 1)):
            work_ref[0, 16 * top + low] = re
            work_ref[1, 16 * top + low] = im
    for top in range(4):
        values = [(work_ref[0, 16 * top + low], work_ref[1, 16 * top + low]) for low in range(16)]
        for low, parts in enumerate(dft16(values, 1)):
            for part in range(2):
                out_ref[16 * top + low, part] = (parts[part] * (1.0 / 64.0)).astype(jnp.bfloat16)


def spectral(x, coulomb):
    count, _, nus, mu = x.shape
    rows = 16
    block = pl.BlockSpec((count, 2, rows, mu), lambda n: (0, 0, n, 0))
    return pl.pallas_call(
        spectral_kernel,
        grid=(nus // rows,),
        in_specs=[block, pl.BlockSpec((count, rows, mu), lambda n: (0, n, 0))],
        out_specs=block,
        out_shape=jax.ShapeDtypeStruct(x.shape, jnp.bfloat16),
        scratch_shapes=[pltpu.VMEM((2, count, rows, mu), jnp.float32)],
        compiler_params=VMEM,
        cost_estimate=pl.CostEstimate(flops=32 * count * nus * mu, bytes_accessed=5 << 19, transcendentals=0),
        name="spectral",
    )(x, coulomb)


def apply_kernel(place_ref, kernel_ref, *refs):
    rights, out_ref = refs[:XS], refs[XS]
    mu, orbitals = out_ref.shape[2:]
    tn = (((0,), (0,)), ((), ()))

    def product(right_ref):
        total = None
        for side in range(2):
            at = (place_ref[0] + side) % ZH
            k_re = kernel_ref[:, at, :, 0, 0].reshape(-1, mu)
            k_im = kernel_ref[:, at, :, 0, 1].reshape(-1, mu)
            b_re = right_ref[:, :, 0, side].reshape(-1, orbitals)
            b_im = right_ref[:, :, 1, side].reshape(-1, orbitals)
            first = jnp.concatenate([k_re, k_im], 1)
            second = jnp.concatenate([-k_im, k_re], 1)
            term = lax.dot_general(first, b_re, tn, preferred_element_type=jnp.float32) + lax.dot_general(
                second, b_im, tn, preferred_element_type=jnp.float32
            )
            total = term if total is None else total + term
        out_ref[0, 0] = total[:mu]
        out_ref[1, 0] = total[mu:]

    for d in range(XS):
        pl.when(pl.program_id(0) == d)(functools.partial(product, rights[d]))


def apply(place, kernel, rights):
    xs, zhs, pairs, kl, _, rows, mu = kernel.shape
    orbitals = rights[0].shape[-1]
    return pl.pallas_call(
        apply_kernel,
        grid_spec=pltpu.PrefetchScalarGridSpec(
            num_scalar_prefetch=1,
            grid=(XS,),
            in_specs=[
                pl.BlockSpec(
                    (xs, zhs, pairs, 1, 2, rows, mu), lambda d, place: (0, 0, 0, (place[1] + XS - d) % XS, 0, 0, 0)
                )
            ]
            + [pl.BlockSpec(rights[0].shape, lambda d, place: (0,) * 6)] * XS,
            out_specs=pl.BlockSpec((2, 1, mu, orbitals), lambda d, place: (0, (place[1] + XS - d) % XS, 0, 0)),
        ),
        out_shape=jax.ShapeDtypeStruct((2, kl, mu, orbitals), jnp.float32),
        compiler_params=VMEM,
        cost_estimate=pl.CostEstimate(
            flops=8 * kl * xs * zhs * pairs * rows * mu * orbitals, bytes_accessed=7 << 20, transcendentals=0
        ),
        name="apply",
    )(place, kernel, *rights)


def swap(blocks, axes):
    return lax.all_to_all(blocks, axes, split_axis=0, concat_axis=0, tiled=True)


def shift(block, d):
    return lax.ppermute(block, "x", [(i, (i + d) % XS) for i in range(XS)])


def on_device(left, right, coulomb):
    parts, kl, nus, orbitals = right.shape
    mu = left.shape[2]
    x = lax.axis_index("x")
    place = jnp.stack([lax.axis_index("zh"), x]).astype(jnp.int32)
    sides = jnp.stack([right, lax.ppermute(right, "zh", [(0, 1), (1, 0)])], 2)
    sides = jnp.broadcast_to(sides.transpose(1, 0, 2, 3, 4)[:, None], (kl, ZQ, parts, 2, nus, orbitals))
    mine = swap(sides.reshape(kl * ZQ, parts, 2, nus, orbitals), ("x", "zq"))
    mine = mine.reshape(XS, ZQ, parts, 2, nus, orbitals)
    lefts = [left]
    for d in range(1, XS):
        block = lax.dynamic_slice_in_dim(left, (x + d) % XS, 1, 1)
        lefts.append(shift(block, d))
    pairs = make_pairs(place, lefts, mine)
    rights = [mine] + [shift(mine, d) for d in range(1, XS)]
    columns = swap(pairs.reshape(KG * XS, parts, 2 * nus, mu), ("kg", "x"))
    columns, rights[1], rights[3] = lax.optimization_barrier((columns, rights[1], rights[3]))
    kernel = swap(spectral(columns, coulomb).reshape(KG, KL, parts, 2 * nus, mu), "kg")
    return apply(place, kernel.reshape(XS, ZH, ZQ // 2, KL, parts, 2 * nus, mu), rights)


def solution(mesh):
    split = Mesh(mesh.devices.reshape(KG, XS, ZH, ZQ), ("kg", "x", "zh", "zq"))
    points = ("x", "zh", "zq")
    in_specs = (P(None, "kg", points, None), P(None, "kg", points, None), P(None, "kg", points))
    out_specs = P(None, "kg", points, None)
    return jax.shard_map(on_device, mesh=split, in_specs=in_specs, out_specs=out_specs, check_vma=False)
```

```python
import functools

import jax
import jax.numpy as jnp
from jax import lax
from jax.experimental import pallas as pl
from jax.experimental.pallas import tpu as pltpu
from jax.sharding import Mesh, PartitionSpec as P

XS, ZH, ZQ = 4, 2, 4
KG, KL = 16, 4
VMEM = pltpu.CompilerParams(vmem_limit_bytes=24 << 20)


def pairs_kernel(place_ref, *refs):
    lefts, right_ref, out_ref = refs[:XS], refs[XS], refs[-1]
    mu, orbitals = lefts[0].shape[2:]
    nt = (((1,), (1,)), ((), ()))
    b_re = right_ref[:, :, 0, 0].reshape(-1, orbitals)
    b_im = right_ref[:, :, 1, 0].reshape(-1, orbitals)
    shape = (XS, ZQ // 2, out_ref.shape[5], mu)
    for d, left_ref in enumerate(lefts):
        a_re, a_im = left_ref[0, 0], left_ref[1, 0]
        first = jnp.concatenate([a_re, a_im], 0)
        second = jnp.concatenate([a_im, -a_re], 0)
        both = lax.dot_general(b_re, first, nt, preferred_element_type=jnp.float32) + lax.dot_general(
            b_im, second, nt, preferred_element_type=jnp.float32
        )
        both = both.astype(jnp.bfloat16)
        at = (place_ref[1] + XS - d) % XS
        out_ref[:, 0, :, at, 0] = both[:, :mu].reshape(shape)
        out_ref[:, 0, :, at, 1] = both[:, mu:].reshape(shape)


def make_pairs(place, lefts, right):
    _, _, mu, orbitals = lefts[0].shape
    nus = right.shape[4]
    one = (2, 1, mu, orbitals)
    left_specs = [pl.BlockSpec(one, lambda side, place: (0, place[1], 0, 0))]
    left_specs += [pl.BlockSpec(one, lambda side, place: (0, 0, 0, 0))] * (XS - 1)
    return pl.pallas_call(
        pairs_kernel,
        grid_spec=pltpu.PrefetchScalarGridSpec(
            num_scalar_prefetch=1,
            grid=(2,),
            in_specs=left_specs
            + [pl.BlockSpec((XS, ZQ, 2, 1, nus, orbitals), lambda side, place: (0, 0, 0, side, 0, 0))],
            out_specs=pl.BlockSpec(
                (XS, 1, ZQ // 2, XS, 2, 2 * nus, mu), lambda side, place: (0, (place[0] + side) % ZH, 0, 0, 0, 0, 0)
            ),
        ),
        out_shape=jax.ShapeDtypeStruct((XS, ZH, ZQ // 2, XS, 2, 2 * nus, mu), jnp.bfloat16),
        compiler_params=VMEM,
        cost_estimate=pl.CostEstimate(
            flops=16 * XS * XS * ZQ * nus * mu * orbitals, bytes_accessed=3 << 20, transcendentals=0
        ),
        name="pairs",
    )(place, *lefts, right)


def dft4(values, sign):
    (r0, i0), (r1, i1), (r2, i2), (r3, i3) = values
    ar, ai, br, bi = r0 + r2, i0 + i2, r0 - r2, i0 - i2
    cr, ci, dr, di = r1 + r3, i1 + i3, r1 - r3, i1 - i3
    if sign < 0:
        return [(ar + cr, ai + ci), (br + di, bi - dr), (ar - cr, ai - ci), (br - di, bi + dr)]
    return [(ar + cr, ai + ci), (br - di, bi + dr), (ar - cr, ai - ci), (br + di, bi - dr)]


def dft16(values, sign):
    out = list(values)
    for slow in range(4):
        out[4 * slow : 4 * slow + 4] = dft4(out[4 * slow : 4 * slow + 4], sign)
    for fast in range(4):
        out[fast::4] = dft4(out[fast::4], sign)
    return out


def spectral_kernel(x_ref, c_ref, out_ref, work_ref):
    for top in range(4):
        values = [
            tuple(x_ref[16 * top + low, part].astype(jnp.float32) for part in range(2)) for low in range(16)
        ]
        for low, (re, im) in enumerate(dft16(values, -1)):
            work_ref[0, 16 * top + low] = re
            work_ref[1, 16 * top + low] = im
    for low in range(16):
        values = [(work_ref[0, 16 * top + low], work_ref[1, 16 * top + low]) for top in range(4)]
        weighted = []
        for top, (re, im) in enumerate(dft4(values, -1)):
            c = c_ref[16 * top + low].astype(jnp.float32)
            weighted.append(tuple((c * part).astype(jnp.bfloat16).astype(jnp.float32) for part in (re, im)))
        for top, (re, im) in enumerate(dft4(weighted, 1)):
            work_ref[0, 16 * top + low] = re
            work_ref[1, 16 * top + low] = im
    for top in range(4):
        values = [(work_ref[0, 16 * top + low], work_ref[1, 16 * top + low]) for low in range(16)]
        for low, parts in enumerate(dft16(values, 1)):
            for part in range(2):
                out_ref[16 * top + low, part] = (parts[part] * (1.0 / 64.0)).astype(jnp.bfloat16)


def spectral(x, coulomb):
    count, _, nus, mu = x.shape
    rows = 16
    block = pl.BlockSpec((count, 2, rows, mu), lambda n: (0, 0, n, 0))
    return pl.pallas_call(
        spectral_kernel,
        grid=(nus // rows,),
        in_specs=[block, pl.BlockSpec((count, rows, mu), lambda n: (0, n, 0))],
        out_specs=block,
        out_shape=jax.ShapeDtypeStruct(x.shape, jnp.bfloat16),
        scratch_shapes=[pltpu.VMEM((2, count, rows, mu), jnp.float32)],
        compiler_params=VMEM,
        cost_estimate=pl.CostEstimate(flops=32 * count * nus * mu, bytes_accessed=5 << 19, transcendentals=0),
        name="spectral",
    )(x, coulomb)


def apply_kernel(sizes, place_ref, kernel_ref, *refs):
    out_ref = refs[-1]
    mu, orbitals = out_ref.shape[2:]
    tn = (((0,), (0,)), ((), ()))

    def product(pieces):
        total = None
        for side in range(2):
            at = (place_ref[0] + side) % ZH
            k_re = kernel_ref[:, at, :, 0, 0].reshape(-1, mu)
            k_im = kernel_ref[:, at, :, 0, 1].reshape(-1, mu)
            b_re, b_im = (
                jnp.concatenate([piece[:, :, part, side].reshape(-1, orbitals) for piece in pieces], 0)
                for part in range(2)
            )
            first = jnp.concatenate([k_re, k_im], 1)
            second = jnp.concatenate([-k_im, k_re], 1)
            term = lax.dot_general(first, b_re, tn, preferred_element_type=jnp.float32) + lax.dot_general(
                second, b_im, tn, preferred_element_type=jnp.float32
            )
            total = term if total is None else total + term
        out_ref[0, 0] = total[:mu]
        out_ref[1, 0] = total[mu:]

    for d in range(XS):
        begin = sum(sizes[:d])
        pl.when(pl.program_id(0) == d)(functools.partial(product, refs[begin : begin + sizes[d]]))


def apply(place, kernel, rights):
    xs, zhs, pairs, kl, _, rows, mu = kernel.shape
    flat = [piece for pieces in rights for piece in pieces]
    orbitals = flat[0].shape[-1]
    return pl.pallas_call(
        functools.partial(apply_kernel, [len(pieces) for pieces in rights]),
        grid_spec=pltpu.PrefetchScalarGridSpec(
            num_scalar_prefetch=1,
            grid=(XS,),
            in_specs=[
                pl.BlockSpec(
                    (xs, zhs, pairs, 1, 2, rows, mu), lambda d, place: (0, 0, 0, (place[1] + XS - d) % XS, 0, 0, 0)
                )
            ]
            + [pl.BlockSpec(piece.shape, lambda d, place: (0,) * 6) for piece in flat],
            out_specs=pl.BlockSpec((2, 1, mu, orbitals), lambda d, place: (0, (place[1] + XS - d) % XS, 0, 0)),
        ),
        out_shape=jax.ShapeDtypeStruct((2, kl, mu, orbitals), jnp.float32),
        compiler_params=VMEM,
        cost_estimate=pl.CostEstimate(
            flops=8 * kl * xs * zhs * pairs * rows * mu * orbitals, bytes_accessed=7 << 20, transcendentals=0
        ),
        name="apply",
    )(place, kernel, *flat)


def swap(blocks, axes):
    return lax.all_to_all(blocks, axes, split_axis=0, concat_axis=0, tiled=True)


def shift(block, d):
    return lax.ppermute(block, "x", [(i, (i + d) % XS) for i in range(XS)])


def on_device(left, right, coulomb):
    parts, kl, nus, orbitals = right.shape
    mu = left.shape[2]
    x = lax.axis_index("x")
    place = jnp.stack([lax.axis_index("zh"), x]).astype(jnp.int32)
    sides = jnp.stack([right, lax.ppermute(right, "zh", [(0, 1), (1, 0)])], 2)
    sides = jnp.broadcast_to(sides.transpose(1, 0, 2, 3, 4)[:, None], (kl, ZQ, parts, 2, nus, orbitals))
    mine = swap(sides.reshape(kl * ZQ, parts, 2, nus, orbitals), ("x", "zq"))
    mine = mine.reshape(XS, ZQ, parts, 2, nus, orbitals)
    lefts = [left]
    for d in range(1, XS):
        block = lax.dynamic_slice_in_dim(left, (x + d) % XS, 1, 1)
        lefts.append(shift(block, d))
    pairs = make_pairs(place, lefts, mine)
    columns = swap(pairs.reshape(KG * XS, parts, 2 * nus, mu), ("kg", "x"))
    low, high = mine[: XS // 2], mine[XS // 2 :]
    columns, up, down = lax.optimization_barrier((columns, shift(low, 1), shift(high, XS - 1)))
    rights = [[mine], [up, shift(high, 1)], [shift(up, 1), shift(down, XS - 1)], [shift(low, XS - 1), down]]
    kernel = swap(spectral(columns, coulomb).reshape(KG, KL, parts, 2 * nus, mu), "kg")
    return apply(place, kernel.reshape(XS, ZH, ZQ // 2, KL, parts, 2 * nus, mu), rights)


def solution(mesh):
    split = Mesh(mesh.devices.reshape(KG, XS, ZH, ZQ), ("kg", "x", "zh", "zq"))
    points = ("x", "zh", "zq")
    in_specs = (P(None, "kg", points, None), P(None, "kg", points, None), P(None, "kg", points))
    out_specs = P(None, "kg", points, None)
    return jax.shard_map(on_device, mesh=split, in_specs=in_specs, out_specs=out_specs, check_vma=False)
```

```python
import functools

import jax
import jax.numpy as jnp
from jax import lax
from jax.experimental import pallas as pl
from jax.experimental.pallas import tpu as pltpu
from jax.sharding import Mesh, PartitionSpec as P

XS, ZH, ZQ = 4, 2, 4
KG, KL = 16, 4
VMEM = pltpu.CompilerParams(vmem_limit_bytes=24 << 20)


def pairs_kernel(place_ref, *refs):
    lefts, right_ref, out_ref = refs[:XS], refs[XS], refs[-1]
    mu, orbitals = lefts[0].shape[2:]
    nt = (((1,), (1,)), ((), ()))
    b_re = right_ref[:, :, 0, 0].reshape(-1, orbitals)
    b_im = right_ref[:, :, 1, 0].reshape(-1, orbitals)
    shape = (XS, ZQ // 2, out_ref.shape[5], mu)
    for d, left_ref in enumerate(lefts):
        a_re, a_im = left_ref[0, 0], left_ref[1, 0]
        first = jnp.concatenate([a_re, a_im], 0)
        second = jnp.concatenate([a_im, -a_re], 0)
        both = lax.dot_general(b_re, first, nt, preferred_element_type=jnp.float32) + lax.dot_general(
            b_im, second, nt, preferred_element_type=jnp.float32
        )
        both = both.astype(jnp.bfloat16)
        at = (place_ref[1] + XS - d) % XS
        out_ref[:, 0, :, at, 0] = both[:, :mu].reshape(shape)
        out_ref[:, 0, :, at, 1] = both[:, mu:].reshape(shape)


def make_pairs(place, lefts, right):
    _, _, mu, orbitals = lefts[0].shape
    nus = right.shape[4]
    one = (2, 1, mu, orbitals)
    left_specs = [pl.BlockSpec(one, lambda side, place: (0, place[1], 0, 0))]
    left_specs += [pl.BlockSpec(one, lambda side, place: (0, 0, 0, 0))] * (XS - 1)
    return pl.pallas_call(
        pairs_kernel,
        grid_spec=pltpu.PrefetchScalarGridSpec(
            num_scalar_prefetch=1,
            grid=(2,),
            in_specs=left_specs
            + [pl.BlockSpec((XS, ZQ, 2, 1, nus, orbitals), lambda side, place: (0, 0, 0, side, 0, 0))],
            out_specs=pl.BlockSpec(
                (XS, 1, ZQ // 2, XS, 2, 2 * nus, mu), lambda side, place: (0, (place[0] + side) % ZH, 0, 0, 0, 0, 0)
            ),
        ),
        out_shape=jax.ShapeDtypeStruct((XS, ZH, ZQ // 2, XS, 2, 2 * nus, mu), jnp.bfloat16),
        compiler_params=VMEM,
        cost_estimate=pl.CostEstimate(
            flops=16 * XS * XS * ZQ * nus * mu * orbitals, bytes_accessed=3 << 20, transcendentals=0
        ),
        name="pairs",
    )(place, *lefts, right)


def dft4(values, sign):
    (r0, i0), (r1, i1), (r2, i2), (r3, i3) = values
    ar, ai, br, bi = r0 + r2, i0 + i2, r0 - r2, i0 - i2
    cr, ci, dr, di = r1 + r3, i1 + i3, r1 - r3, i1 - i3
    if sign < 0:
        return [(ar + cr, ai + ci), (br + di, bi - dr), (ar - cr, ai - ci), (br - di, bi + dr)]
    return [(ar + cr, ai + ci), (br - di, bi + dr), (ar - cr, ai - ci), (br + di, bi - dr)]


def dft16(values, sign):
    out = list(values)
    for slow in range(4):
        out[4 * slow : 4 * slow + 4] = dft4(out[4 * slow : 4 * slow + 4], sign)
    for fast in range(4):
        out[fast::4] = dft4(out[fast::4], sign)
    return out


def spectral_kernel(x_ref, c_ref, out_ref, work_ref):
    for top in range(4):
        values = [
            tuple(x_ref[16 * top + low, part].astype(jnp.float32) for part in range(2)) for low in range(16)
        ]
        for low, (re, im) in enumerate(dft16(values, -1)):
            work_ref[0, 16 * top + low] = re
            work_ref[1, 16 * top + low] = im
    for low in range(16):
        values = [(work_ref[0, 16 * top + low], work_ref[1, 16 * top + low]) for top in range(4)]
        weighted = []
        for top, (re, im) in enumerate(dft4(values, -1)):
            c = c_ref[16 * top + low].astype(jnp.float32)
            weighted.append(tuple((c * part).astype(jnp.bfloat16).astype(jnp.float32) for part in (re, im)))
        for top, (re, im) in enumerate(dft4(weighted, 1)):
            work_ref[0, 16 * top + low] = re
            work_ref[1, 16 * top + low] = im
    for top in range(4):
        values = [(work_ref[0, 16 * top + low], work_ref[1, 16 * top + low]) for low in range(16)]
        for low, parts in enumerate(dft16(values, 1)):
            for part in range(2):
                out_ref[16 * top + low, part] = (parts[part] * (1.0 / 64.0)).astype(jnp.bfloat16)


def spectral(x, coulomb):
    count, _, nus, mu = x.shape
    rows = 16
    block = pl.BlockSpec((count, 2, rows, mu), lambda n: (0, 0, n, 0))
    return pl.pallas_call(
        spectral_kernel,
        grid=(nus // rows,),
        in_specs=[block, pl.BlockSpec((count, rows, mu), lambda n: (0, n, 0))],
        out_specs=block,
        out_shape=jax.ShapeDtypeStruct(x.shape, jnp.bfloat16),
        scratch_shapes=[pltpu.VMEM((2, count, rows, mu), jnp.float32)],
        compiler_params=VMEM,
        cost_estimate=pl.CostEstimate(flops=32 * count * nus * mu, bytes_accessed=5 << 19, transcendentals=0),
        name="spectral",
    )(x, coulomb)


def apply_kernel(plan, place_ref, kernel_ref, *refs):
    out_ref, right_ref, sems = refs[-3:]
    mu, orbitals = out_ref.shape[2:]
    tn = (((0,), (0,)), ((), ()))
    copies = [[] for _ in plan]
    n = 0
    for d, pieces in enumerate(plan):
        at = 0
        for array, begin, length in pieces:
            source = refs[array].at[pl.ds(begin, length)]
            copies[d].append(pltpu.make_async_copy(source, right_ref.at[d, pl.ds(at, length)], sems.at[n]))
            at += length
            n += 1

    @pl.when(pl.program_id(0) == 0)
    def _():
        for copy in copies[0] + copies[1]:
            copy.start()

    def step(d):
        for copy in copies[d + 2] if d + 2 < XS else []:
            copy.start()
        for copy in copies[d]:
            copy.wait()
        total = None
        for side in range(2):
            at = (place_ref[0] + side) % ZH
            k_re = kernel_ref[:, at, :, 0, 0].reshape(-1, mu)
            k_im = kernel_ref[:, at, :, 0, 1].reshape(-1, mu)
            b_re = right_ref[d, :, :, 0, side].reshape(-1, orbitals)
            b_im = right_ref[d, :, :, 1, side].reshape(-1, orbitals)
            first = jnp.concatenate([k_re, k_im], 1)
            second = jnp.concatenate([-k_im, k_re], 1)
            term = lax.dot_general(first, b_re, tn, preferred_element_type=jnp.float32) + lax.dot_general(
                second, b_im, tn, preferred_element_type=jnp.float32
            )
            total = term if total is None else total + term
        out_ref[0, 0] = total[:mu]
        out_ref[1, 0] = total[mu:]

    for d in range(XS):
        pl.when(pl.program_id(0) == d)(functools.partial(step, d))


def apply(place, kernel, arrays, plan):
    xs, zhs, pairs, kl, _, rows, mu = kernel.shape
    orbitals = arrays[0].shape[-1]
    return pl.pallas_call(
        functools.partial(apply_kernel, plan),
        grid_spec=pltpu.PrefetchScalarGridSpec(
            num_scalar_prefetch=1,
            grid=(XS,),
            in_specs=[
                pl.BlockSpec(
                    (xs, zhs, pairs, 1, 2, rows, mu), lambda d, place: (0, 0, 0, (place[1] + XS - d) % XS, 0, 0, 0)
                )
            ]
            + [pl.BlockSpec(memory_space=pl.ANY)] * len(arrays),
            out_specs=pl.BlockSpec((2, 1, mu, orbitals), lambda d, place: (0, (place[1] + XS - d) % XS, 0, 0)),
            scratch_shapes=[
                pltpu.VMEM((XS, XS, *arrays[0].shape[1:]), jnp.bfloat16),
                pltpu.SemaphoreType.DMA((sum(map(len, plan)),)),
            ],
        ),
        out_shape=jax.ShapeDtypeStruct((2, kl, mu, orbitals), jnp.float32),
        compiler_params=VMEM,
        cost_estimate=pl.CostEstimate(
            flops=8 * kl * xs * zhs * pairs * rows * mu * orbitals, bytes_accessed=7 << 20, transcendentals=0
        ),
        name="apply",
    )(place, kernel, *arrays)


def swap(blocks, axes):
    return lax.all_to_all(blocks, axes, split_axis=0, concat_axis=0, tiled=True)


def shift(block, d):
    return lax.ppermute(block, "x", [(i, (i + d) % XS) for i in range(XS)])


def on_device(left, right, coulomb):
    parts, kl, nus, orbitals = right.shape
    mu = left.shape[2]
    x = lax.axis_index("x")
    place = jnp.stack([lax.axis_index("zh"), x]).astype(jnp.int32)
    sides = jnp.stack([right, lax.ppermute(right, "zh", [(0, 1), (1, 0)])], 2)
    sides = jnp.broadcast_to(sides.transpose(1, 0, 2, 3, 4)[:, None], (kl, ZQ, parts, 2, nus, orbitals))
    mine = swap(sides.reshape(kl * ZQ, parts, 2, nus, orbitals), ("x", "zq"))
    mine = mine.reshape(XS, ZQ, parts, 2, nus, orbitals)
    lefts = [left]
    for d in range(1, XS):
        block = lax.dynamic_slice_in_dim(left, (x + d) % XS, 1, 1)
        lefts.append(shift(block, d))
    pairs = make_pairs(place, lefts, mine)
    columns = swap(pairs.reshape(KG * XS, parts, 2 * nus, mu), ("kg", "x"))
    low, high = mine[: XS // 2], mine[XS // 2 :]
    spatial = spectral(columns, coulomb)
    spatial, up, down = lax.optimization_barrier((spatial, shift(low, 1), shift(high, XS - 1)))
    late = jnp.concatenate([shift(high, 1), shift(up, 1), shift(down, XS - 1), shift(low, XS - 1)])
    half = XS // 2
    plan = [
        [(0, 0, XS)],
        [(1, 0, half), (3, 0, half)],
        [(3, half, XS)],
        [(3, half + XS, half), (2, 0, half)],
    ]
    kernel = swap(spatial.reshape(KG, KL, parts, 2 * nus, mu), "kg")
    return apply(place, kernel.reshape(XS, ZH, ZQ // 2, KL, parts, 2 * nus, mu), [mine, up, down, late], plan)


def solution(mesh):
    split = Mesh(mesh.devices.reshape(KG, XS, ZH, ZQ), ("kg", "x", "zh", "zq"))
    points = ("x", "zh", "zq")
    in_specs = (P(None, "kg", points, None), P(None, "kg", points, None), P(None, "kg", points))
    out_specs = P(None, "kg", points, None)
    return jax.shard_map(on_device, mesh=split, in_specs=in_specs, out_specs=out_specs, check_vma=False)
```

```python
import functools

import jax
import jax.numpy as jnp
from jax import lax
from jax.experimental import pallas as pl
from jax.experimental.pallas import tpu as pltpu
from jax.sharding import Mesh, PartitionSpec as P

XS, ZH, ZQ = 4, 2, 4
KG, KL = 16, 4
VMEM = pltpu.CompilerParams(vmem_limit_bytes=24 << 20)


def send_kernel(right_ref, *refs):
    out_ref = refs[-1]
    for part in range(2):
        block = right_ref[part]
        for zq in range(ZQ):
            out_ref[:, zq, part, 0] = block


def make_send(right, side, base=None):
    parts, kl, nus, orbitals = right.shape
    more = [] if base is None else [base]
    return pl.pallas_call(
        send_kernel,
        grid=(1,),
        in_specs=[pl.BlockSpec(right.shape, lambda n: (0, 0, 0, 0))] + [pl.BlockSpec(memory_space=pl.ANY)] * len(more),
        out_specs=pl.BlockSpec((kl, ZQ, parts, 1, nus, orbitals), lambda n: (0, 0, 0, side, 0, 0)),
        out_shape=jax.ShapeDtypeStruct((kl, ZQ, parts, 2, nus, orbitals), right.dtype),
        input_output_aliases={1: 0} if more else {},
        compiler_params=VMEM,
        cost_estimate=pl.CostEstimate(flops=0, bytes_accessed=5 << 17, transcendentals=0),
        name="send",
    )(right, *more)


def pairs_kernel(place_ref, *refs):
    lefts, right_ref, out_ref = refs[:XS], refs[XS], refs[-1]
    mu, orbitals = lefts[0].shape[2:]
    nt = (((1,), (1,)), ((), ()))
    b_re = right_ref[:, :, 0, 0].reshape(-1, orbitals)
    b_im = right_ref[:, :, 1, 0].reshape(-1, orbitals)
    shape = (XS, ZQ // 2, out_ref.shape[5], mu)
    for d, left_ref in enumerate(lefts):
        a_re, a_im = left_ref[0, 0], left_ref[1, 0]
        first = jnp.concatenate([a_re, a_im], 0)
        second = jnp.concatenate([a_im, -a_re], 0)
        both = lax.dot_general(b_re, first, nt, preferred_element_type=jnp.float32) + lax.dot_general(
            b_im, second, nt, preferred_element_type=jnp.float32
        )
        both = both.astype(jnp.bfloat16)
        at = (place_ref[1] + XS - d) % XS
        out_ref[:, 0, :, at, 0] = both[:, :mu].reshape(shape)
        out_ref[:, 0, :, at, 1] = both[:, mu:].reshape(shape)


def make_pairs(place, lefts, right):
    _, _, mu, orbitals = lefts[0].shape
    nus = right.shape[4]
    one = (2, 1, mu, orbitals)
    left_specs = [pl.BlockSpec(one, lambda side, place: (0, place[1], 0, 0))]
    left_specs += [pl.BlockSpec(one, lambda side, place: (0, 0, 0, 0))] * (XS - 1)
    return pl.pallas_call(
        pairs_kernel,
        grid_spec=pltpu.PrefetchScalarGridSpec(
            num_scalar_prefetch=1,
            grid=(2,),
            in_specs=left_specs
            + [pl.BlockSpec((XS, ZQ, 2, 1, nus, orbitals), lambda side, place: (0, 0, 0, side, 0, 0))],
            out_specs=pl.BlockSpec(
                (XS, 1, ZQ // 2, XS, 2, 2 * nus, mu), lambda side, place: (0, (place[0] + side) % ZH, 0, 0, 0, 0, 0)
            ),
        ),
        out_shape=jax.ShapeDtypeStruct((XS, ZH, ZQ // 2, XS, 2, 2 * nus, mu), jnp.bfloat16),
        compiler_params=VMEM,
        cost_estimate=pl.CostEstimate(
            flops=16 * XS * XS * ZQ * nus * mu * orbitals, bytes_accessed=3 << 20, transcendentals=0
        ),
        name="pairs",
    )(place, *lefts, right)


def dft4(values, sign):
    (r0, i0), (r1, i1), (r2, i2), (r3, i3) = values
    ar, ai, br, bi = r0 + r2, i0 + i2, r0 - r2, i0 - i2
    cr, ci, dr, di = r1 + r3, i1 + i3, r1 - r3, i1 - i3
    if sign < 0:
        return [(ar + cr, ai + ci), (br + di, bi - dr), (ar - cr, ai - ci), (br - di, bi + dr)]
    return [(ar + cr, ai + ci), (br - di, bi + dr), (ar - cr, ai - ci), (br + di, bi - dr)]


def dft16(values, sign):
    out = list(values)
    for slow in range(4):
        out[4 * slow : 4 * slow + 4] = dft4(out[4 * slow : 4 * slow + 4], sign)
    for fast in range(4):
        out[fast::4] = dft4(out[fast::4], sign)
    return out


def spectral_kernel(x_ref, c_ref, out_ref, work_ref):
    for top in range(4):
        values = [
            tuple(x_ref[16 * top + low, part].astype(jnp.float32) for part in range(2)) for low in range(16)
        ]
        for low, (re, im) in enumerate(dft16(values, -1)):
            work_ref[0, 16 * top + low] = re
            work_ref[1, 16 * top + low] = im
    for low in range(16):
        values = [(work_ref[0, 16 * top + low], work_ref[1, 16 * top + low]) for top in range(4)]
        weighted = []
        for top, (re, im) in enumerate(dft4(values, -1)):
            c = c_ref[16 * top + low].astype(jnp.float32)
            weighted.append(tuple((c * part).astype(jnp.bfloat16).astype(jnp.float32) for part in (re, im)))
        for top, (re, im) in enumerate(dft4(weighted, 1)):
            work_ref[0, 16 * top + low] = re
            work_ref[1, 16 * top + low] = im
    for top in range(4):
        values = [(work_ref[0, 16 * top + low], work_ref[1, 16 * top + low]) for low in range(16)]
        for low, parts in enumerate(dft16(values, 1)):
            for part in range(2):
                out_ref[16 * top + low, part] = (parts[part] * (1.0 / 64.0)).astype(jnp.bfloat16)


def spectral(x, coulomb):
    count, _, nus, mu = x.shape
    rows = 16
    block = pl.BlockSpec((count, 2, rows, mu), lambda n: (0, 0, n, 0))
    return pl.pallas_call(
        spectral_kernel,
        grid=(nus // rows,),
        in_specs=[block, pl.BlockSpec((count, rows, mu), lambda n: (0, n, 0))],
        out_specs=block,
        out_shape=jax.ShapeDtypeStruct(x.shape, jnp.bfloat16),
        scratch_shapes=[pltpu.VMEM((2, count, rows, mu), jnp.float32)],
        compiler_params=VMEM,
        cost_estimate=pl.CostEstimate(flops=32 * count * nus * mu, bytes_accessed=5 << 19, transcendentals=0),
        name="spectral",
    )(x, coulomb)


def apply_kernel(plan, place_ref, kernel_ref, *refs):
    out_ref, right_ref, sems = refs[-3:]
    mu, orbitals = out_ref.shape[2:]
    tn = (((0,), (0,)), ((), ()))
    copies = [[] for _ in plan]
    n = 0
    for d, pieces in enumerate(plan):
        at = 0
        for array, begin, length in pieces:
            source = refs[array].at[pl.ds(begin, length)]
            copies[d].append(pltpu.make_async_copy(source, right_ref.at[d, pl.ds(at, length)], sems.at[n]))
            at += length
            n += 1

    @pl.when(pl.program_id(0) == 0)
    def _():
        for copy in copies[0] + copies[1]:
            copy.start()

    def step(d):
        for copy in copies[d + 2] if d + 2 < XS else []:
            copy.start()
        for copy in copies[d]:
            copy.wait()
        total = None
        for side in range(2):
            at = (place_ref[0] + side) % ZH
            k_re = kernel_ref[:, at, :, 0, 0].reshape(-1, mu)
            k_im = kernel_ref[:, at, :, 0, 1].reshape(-1, mu)
            b_re = right_ref[d, :, :, 0, side].reshape(-1, orbitals)
            b_im = right_ref[d, :, :, 1, side].reshape(-1, orbitals)
            first = jnp.concatenate([k_re, k_im], 1)
            second = jnp.concatenate([-k_im, k_re], 1)
            term = lax.dot_general(first, b_re, tn, preferred_element_type=jnp.float32) + lax.dot_general(
                second, b_im, tn, preferred_element_type=jnp.float32
            )
            total = term if total is None else total + term
        out_ref[0, 0] = total[:mu]
        out_ref[1, 0] = total[mu:]

    for d in range(XS):
        pl.when(pl.program_id(0) == d)(functools.partial(step, d))


def apply(place, kernel, arrays, plan):
    xs, zhs, pairs, kl, _, rows, mu = kernel.shape
    orbitals = arrays[0].shape[-1]
    return pl.pallas_call(
        functools.partial(apply_kernel, plan),
        grid_spec=pltpu.PrefetchScalarGridSpec(
            num_scalar_prefetch=1,
            grid=(XS,),
            in_specs=[
                pl.BlockSpec(
                    (xs, zhs, pairs, 1, 2, rows, mu), lambda d, place: (0, 0, 0, (place[1] + XS - d) % XS, 0, 0, 0)
                )
            ]
            + [pl.BlockSpec(memory_space=pl.ANY)] * len(arrays),
            out_specs=pl.BlockSpec((2, 1, mu, orbitals), lambda d, place: (0, (place[1] + XS - d) % XS, 0, 0)),
            scratch_shapes=[
                pltpu.VMEM((XS, XS, *arrays[0].shape[1:]), jnp.bfloat16),
                pltpu.SemaphoreType.DMA((sum(map(len, plan)),)),
            ],
        ),
        out_shape=jax.ShapeDtypeStruct((2, kl, mu, orbitals), jnp.float32),
        compiler_params=VMEM,
        cost_estimate=pl.CostEstimate(
            flops=8 * kl * xs * zhs * pairs * rows * mu * orbitals, bytes_accessed=7 << 20, transcendentals=0
        ),
        name="apply",
    )(place, kernel, *arrays)


def swap(blocks, axes):
    return lax.all_to_all(blocks, axes, split_axis=0, concat_axis=0, tiled=True)


def shift(block, d):
    return lax.ppermute(block, "x", [(i, (i + d) % XS) for i in range(XS)])


def on_device(left, right, coulomb):
    parts, kl, nus, orbitals = right.shape
    mu = left.shape[2]
    x = lax.axis_index("x")
    place = jnp.stack([lax.axis_index("zh"), x]).astype(jnp.int32)
    other = lax.ppermute(right, "zh", [(0, 1), (1, 0)])
    sides = make_send(other, 1, make_send(right, 0))
    mine = swap(sides.reshape(kl * ZQ, parts, 2, nus, orbitals), ("x", "zq"))
    mine = mine.reshape(XS, ZQ, parts, 2, nus, orbitals)
    lefts = [left]
    for d in range(1, XS):
        block = lax.dynamic_slice_in_dim(left, (x + d) % XS, 1, 1)
        lefts.append(shift(block, d))
    pairs = make_pairs(place, lefts, mine)
    columns = swap(pairs.reshape(KG * XS, parts, 2 * nus, mu), ("kg", "x"))
    low, high = mine[: XS // 2], mine[XS // 2 :]
    spatial = spectral(columns, coulomb)
    spatial, up, down = lax.optimization_barrier((spatial, shift(low, 1), shift(high, XS - 1)))
    late = jnp.concatenate([shift(high, 1), shift(up, 1), shift(down, XS - 1), shift(low, XS - 1)])
    half = XS // 2
    plan = [
        [(0, 0, XS)],
        [(1, 0, half), (3, 0, half)],
        [(3, half, XS)],
        [(3, half + XS, half), (2, 0, half)],
    ]
    kernel = swap(spatial.reshape(KG, KL, parts, 2 * nus, mu), "kg")
    return apply(place, kernel.reshape(XS, ZH, ZQ // 2, KL, parts, 2 * nus, mu), [mine, up, down, late], plan)


def solution(mesh):
    split = Mesh(mesh.devices.reshape(KG, XS, ZH, ZQ), ("kg", "x", "zh", "zq"))
    points = ("x", "zh", "zq")
    in_specs = (P(None, "kg", points, None), P(None, "kg", points, None), P(None, "kg", points))
    out_specs = P(None, "kg", points, None)
    return jax.shard_map(on_device, mesh=split, in_specs=in_specs, out_specs=out_specs, check_vma=False)
```

```python
import functools

import jax
import jax.numpy as jnp
from jax import lax
from jax.experimental import pallas as pl
from jax.experimental.pallas import tpu as pltpu
from jax.sharding import Mesh, PartitionSpec as P

XS, ZH, ZQ = 4, 2, 4
KG, KL = 16, 4
VMEM = pltpu.CompilerParams(vmem_limit_bytes=24 << 20)


def send_kernel(right_ref, *refs):
    out_ref = refs[-1]
    for part in range(2):
        block = right_ref[part]
        for zq in range(ZQ):
            out_ref[:, zq, part, 0] = block


def make_send(right, side, base=None):
    parts, kl, nus, orbitals = right.shape
    more = [] if base is None else [base]
    return pl.pallas_call(
        send_kernel,
        grid=(1,),
        in_specs=[pl.BlockSpec(right.shape, lambda n: (0, 0, 0, 0))] + [pl.BlockSpec(memory_space=pl.ANY)] * len(more),
        out_specs=pl.BlockSpec((kl, ZQ, parts, 1, nus, orbitals), lambda n: (0, 0, 0, side, 0, 0)),
        out_shape=jax.ShapeDtypeStruct((kl, ZQ, parts, 2, nus, orbitals), right.dtype),
        input_output_aliases={1: 0} if more else {},
        compiler_params=VMEM,
        cost_estimate=pl.CostEstimate(flops=0, bytes_accessed=5 << 17, transcendentals=0),
        name="send",
    )(right, *more)


def pairs_kernel(place_ref, *refs):
    lefts, (right_ref, out_ref, done_ref, sems) = refs[:XS], refs[XS:]
    mu, orbitals = lefts[0].shape[2:]
    nt = (((1,), (1,)), ((), ()))
    shape = (XS, ZQ // 2, done_ref.shape[5], mu)
    copies = []
    for side in range(2):
        b_re = right_ref[:, :, 0, side].reshape(-1, orbitals)
        b_im = right_ref[:, :, 1, side].reshape(-1, orbitals)
        for d, left_ref in enumerate(lefts):
            a_re, a_im = left_ref[0, 0], left_ref[1, 0]
            first = jnp.concatenate([a_re, a_im], 0)
            second = jnp.concatenate([a_im, -a_re], 0)
            both = lax.dot_general(b_re, first, nt, preferred_element_type=jnp.float32) + lax.dot_general(
                b_im, second, nt, preferred_element_type=jnp.float32
            )
            both = both.astype(jnp.bfloat16)
            at = (place_ref[1] + XS - d) % XS
            done_ref[side, :, :, at, 0] = both[:, :mu].reshape(shape)
            done_ref[side, :, :, at, 1] = both[:, mu:].reshape(shape)
        copies.append(
            pltpu.make_async_copy(done_ref.at[side], out_ref.at[:, (place_ref[0] + side) % ZH], sems.at[side])
        )
        copies[-1].start()
    for copy in copies:
        copy.wait()


def make_pairs(place, lefts, right):
    _, _, mu, orbitals = lefts[0].shape
    nus = right.shape[4]
    half = (XS, ZQ // 2, XS, 2, 2 * nus, mu)
    return pl.pallas_call(
        pairs_kernel,
        grid_spec=pltpu.PrefetchScalarGridSpec(
            num_scalar_prefetch=1,
            grid=(1,),
            in_specs=[pl.BlockSpec((2, 1, mu, orbitals), lambda n, place: (0, place[1], 0, 0))]
            + [pl.BlockSpec(memory_space=pltpu.VMEM)] * XS,
            out_specs=pl.BlockSpec(memory_space=pl.ANY),
            scratch_shapes=[pltpu.VMEM((2, *half), jnp.bfloat16), pltpu.SemaphoreType.DMA((2,))],
        ),
        out_shape=jax.ShapeDtypeStruct((XS, ZH, *half[1:]), jnp.bfloat16),
        compiler_params=VMEM,
        cost_estimate=pl.CostEstimate(
            flops=16 * XS * XS * ZQ * nus * mu * orbitals, bytes_accessed=3 << 20, transcendentals=0
        ),
        name="pairs",
    )(place, *lefts, right)


def dft4(values, sign):
    (r0, i0), (r1, i1), (r2, i2), (r3, i3) = values
    ar, ai, br, bi = r0 + r2, i0 + i2, r0 - r2, i0 - i2
    cr, ci, dr, di = r1 + r3, i1 + i3, r1 - r3, i1 - i3
    if sign < 0:
        return [(ar + cr, ai + ci), (br + di, bi - dr), (ar - cr, ai - ci), (br - di, bi + dr)]
    return [(ar + cr, ai + ci), (br - di, bi + dr), (ar - cr, ai - ci), (br + di, bi - dr)]


def dft16(values, sign):
    out = list(values)
    for slow in range(4):
        out[4 * slow : 4 * slow + 4] = dft4(out[4 * slow : 4 * slow + 4], sign)
    for fast in range(4):
        out[fast::4] = dft4(out[fast::4], sign)
    return out


def spectral_kernel(x_ref, c_ref, out_ref, work_ref):
    for top in range(4):
        values = [
            tuple(x_ref[16 * top + low, part].astype(jnp.float32) for part in range(2)) for low in range(16)
        ]
        for low, (re, im) in enumerate(dft16(values, -1)):
            work_ref[0, 16 * top + low] = re
            work_ref[1, 16 * top + low] = im
    for low in range(16):
        values = [(work_ref[0, 16 * top + low], work_ref[1, 16 * top + low]) for top in range(4)]
        weighted = []
        for top, (re, im) in enumerate(dft4(values, -1)):
            c = c_ref[16 * top + low].astype(jnp.float32)
            weighted.append(tuple((c * part).astype(jnp.bfloat16).astype(jnp.float32) for part in (re, im)))
        for top, (re, im) in enumerate(dft4(weighted, 1)):
            work_ref[0, 16 * top + low] = re
            work_ref[1, 16 * top + low] = im
    for top in range(4):
        values = [(work_ref[0, 16 * top + low], work_ref[1, 16 * top + low]) for low in range(16)]
        for low, parts in enumerate(dft16(values, 1)):
            for part in range(2):
                out_ref[16 * top + low, part] = (parts[part] * (1.0 / 64.0)).astype(jnp.bfloat16)


def spectral(x, coulomb):
    count, _, nus, mu = x.shape
    rows = 16
    block = pl.BlockSpec((count, 2, rows, mu), lambda n: (0, 0, n, 0))
    return pl.pallas_call(
        spectral_kernel,
        grid=(nus // rows,),
        in_specs=[block, pl.BlockSpec((count, rows, mu), lambda n: (0, n, 0))],
        out_specs=block,
        out_shape=jax.ShapeDtypeStruct(x.shape, jnp.bfloat16),
        scratch_shapes=[pltpu.VMEM((2, count, rows, mu), jnp.float32)],
        compiler_params=VMEM,
        cost_estimate=pl.CostEstimate(flops=32 * count * nus * mu, bytes_accessed=5 << 19, transcendentals=0),
        name="spectral",
    )(x, coulomb)


def apply_kernel(plan, place_ref, kernel_ref, *refs):
    out_ref, blocks_ref, right_ref, done_ref, in_sems, out_sems = refs[-6:]
    mu, orbitals = out_ref.shape[2:]
    tn = (((0,), (0,)), ((), ()))
    gets, puts = [], []
    n = 0
    for d, pieces in enumerate(plan):
        k = (place_ref[1] + XS - d) % XS
        gets.append([pltpu.make_async_copy(kernel_ref.at[:, :, :, k], blocks_ref.at[d], in_sems.at[n])])
        n += 1
        at = 0
        for array, begin, length in pieces:
            source = refs[array].at[pl.ds(begin, length)]
            gets[d].append(pltpu.make_async_copy(source, right_ref.at[d, pl.ds(at, length)], in_sems.at[n]))
            at += length
            n += 1
        puts.append(pltpu.make_async_copy(done_ref.at[d], out_ref.at[:, k], out_sems.at[d]))
    for copy in gets[0] + gets[1]:
        copy.start()
    for d in range(XS):
        for copy in gets[d + 2] if d + 2 < XS else []:
            copy.start()
        for copy in gets[d]:
            copy.wait()
        total = None
        for side in range(2):
            at = (place_ref[0] + side) % ZH
            k_re = blocks_ref[d, :, at, :, 0].reshape(-1, mu)
            k_im = blocks_ref[d, :, at, :, 1].reshape(-1, mu)
            b_re = right_ref[d, :, :, 0, side].reshape(-1, orbitals)
            b_im = right_ref[d, :, :, 1, side].reshape(-1, orbitals)
            first = jnp.concatenate([k_re, k_im], 1)
            second = jnp.concatenate([-k_im, k_re], 1)
            term = lax.dot_general(first, b_re, tn, preferred_element_type=jnp.float32) + lax.dot_general(
                second, b_im, tn, preferred_element_type=jnp.float32
            )
            total = term if total is None else total + term
        done_ref[d, 0] = total[:mu]
        done_ref[d, 1] = total[mu:]
        puts[d].start()
    for copy in puts:
        copy.wait()


def apply(place, kernel, arrays, plan):
    xs, zhs, pairs, kl, _, rows, mu = kernel.shape
    orbitals = arrays[0].shape[-1]
    return pl.pallas_call(
        functools.partial(apply_kernel, plan),
        grid_spec=pltpu.PrefetchScalarGridSpec(
            num_scalar_prefetch=1,
            grid=(1,),
            in_specs=[pl.BlockSpec(memory_space=pl.ANY)] * (1 + len(arrays)),
            out_specs=pl.BlockSpec(memory_space=pl.ANY),
            scratch_shapes=[
                pltpu.VMEM((XS, xs, zhs, pairs, 2, rows, mu), jnp.bfloat16),
                pltpu.VMEM((XS, XS, *arrays[0].shape[1:]), jnp.bfloat16),
                pltpu.VMEM((XS, 2, mu, orbitals), jnp.float32),
                pltpu.SemaphoreType.DMA((XS + sum(map(len, plan)),)),
                pltpu.SemaphoreType.DMA((XS,)),
            ],
        ),
        out_shape=jax.ShapeDtypeStruct((2, kl, mu, orbitals), jnp.float32),
        compiler_params=VMEM,
        cost_estimate=pl.CostEstimate(
            flops=8 * kl * xs * zhs * pairs * rows * mu * orbitals, bytes_accessed=7 << 20, transcendentals=0
        ),
        name="apply",
    )(place, kernel, *arrays)


def swap(blocks, axes):
    return lax.all_to_all(blocks, axes, split_axis=0, concat_axis=0, tiled=True)


def shift(block, d):
    return lax.ppermute(block, "x", [(i, (i + d) % XS) for i in range(XS)])


def on_device(left, right, coulomb):
    parts, kl, nus, orbitals = right.shape
    mu = left.shape[2]
    x = lax.axis_index("x")
    place = jnp.stack([lax.axis_index("zh"), x]).astype(jnp.int32)
    other = lax.ppermute(right, "zh", [(0, 1), (1, 0)])
    sides = make_send(other, 1, make_send(right, 0))
    mine = swap(sides.reshape(kl * ZQ, parts, 2, nus, orbitals), ("x", "zq"))
    mine = mine.reshape(XS, ZQ, parts, 2, nus, orbitals)
    lefts = [left]
    for d in range(1, XS):
        block = lax.dynamic_slice_in_dim(left, (x + d) % XS, 1, 1)
        lefts.append(shift(block, d))
    pairs = make_pairs(place, lefts, mine)
    columns = swap(pairs.reshape(KG * XS, parts, 2 * nus, mu), ("kg", "x"))
    low, high = mine[: XS // 2], mine[XS // 2 :]
    spatial = spectral(columns, coulomb)
    spatial, up, down = lax.optimization_barrier((spatial, shift(low, 1), shift(high, XS - 1)))
    late = jnp.concatenate([shift(high, 1), shift(up, 1), shift(down, XS - 1), shift(low, XS - 1)])
    half = XS // 2
    plan = [
        [(0, 0, XS)],
        [(1, 0, half), (3, 0, half)],
        [(3, half, XS)],
        [(3, half + XS, half), (2, 0, half)],
    ]
    kernel = swap(spatial.reshape(KG, KL, parts, 2 * nus, mu), "kg")
    return apply(place, kernel.reshape(XS, ZH, ZQ // 2, KL, parts, 2 * nus, mu), [mine, up, down, late], plan)


def solution(mesh):
    split = Mesh(mesh.devices.reshape(KG, XS, ZH, ZQ), ("kg", "x", "zh", "zq"))
    points = ("x", "zh", "zq")
    in_specs = (P(None, "kg", points, None), P(None, "kg", points, None), P(None, "kg", points))
    out_specs = P(None, "kg", points, None)
    return jax.shard_map(on_device, mesh=split, in_specs=in_specs, out_specs=out_specs, check_vma=False)
```

```python
import functools

import jax
import jax.numpy as jnp
from jax import lax
from jax.experimental import pallas as pl
from jax.experimental.pallas import tpu as pltpu
from jax.sharding import Mesh, PartitionSpec as P

XS, ZH, ZQ = 4, 2, 4
KG, KL = 16, 4
VMEM = pltpu.CompilerParams(vmem_limit_bytes=24 << 20)


def send_kernel(right_ref, *refs):
    out_ref = refs[-1]
    for part in range(2):
        block = right_ref[part]
        for zq in range(ZQ):
            out_ref[:, zq, part, 0] = block


def make_send(right, side, base=None):
    parts, kl, nus, orbitals = right.shape
    more = [] if base is None else [base]
    return pl.pallas_call(
        send_kernel,
        grid=(1,),
        in_specs=[pl.BlockSpec(right.shape, lambda n: (0, 0, 0, 0))] + [pl.BlockSpec(memory_space=pl.ANY)] * len(more),
        out_specs=pl.BlockSpec((kl, ZQ, parts, 1, nus, orbitals), lambda n: (0, 0, 0, side, 0, 0)),
        out_shape=jax.ShapeDtypeStruct((kl, ZQ, parts, 2, nus, orbitals), right.dtype),
        input_output_aliases={1: 0} if more else {},
        compiler_params=VMEM,
        cost_estimate=pl.CostEstimate(flops=0, bytes_accessed=5 << 17, transcendentals=0),
        name="send",
    )(right, *more)


def pairs_kernel(place_ref, *refs):
    lefts, (right_ref, out_ref, done_ref, sems) = refs[:XS], refs[XS:]
    mu, orbitals = lefts[0].shape[2:]
    nt = (((1,), (1,)), ((), ()))
    shape = (XS, ZQ // 2, done_ref.shape[5], mu)
    copies = []
    for side in range(2):
        b_re = right_ref[:, :, 0, side].reshape(-1, orbitals)
        b_im = right_ref[:, :, 1, side].reshape(-1, orbitals)
        for d, left_ref in enumerate(lefts):
            a_re, a_im = left_ref[0, 0], left_ref[1, 0]
            first = jnp.concatenate([a_re, a_im], 0)
            second = jnp.concatenate([a_im, -a_re], 0)
            both = lax.dot_general(b_re, first, nt, preferred_element_type=jnp.float32) + lax.dot_general(
                b_im, second, nt, preferred_element_type=jnp.float32
            )
            both = both.astype(jnp.bfloat16)
            at = (place_ref[1] + XS - d) % XS
            done_ref[side, :, :, at, 0] = both[:, :mu].reshape(shape)
            done_ref[side, :, :, at, 1] = both[:, mu:].reshape(shape)
        copies.append(
            pltpu.make_async_copy(done_ref.at[side], out_ref.at[:, (place_ref[0] + side) % ZH], sems.at[side])
        )
        copies[-1].start()
    for copy in copies:
        copy.wait()


def make_pairs(place, lefts, right):
    _, _, mu, orbitals = lefts[0].shape
    nus = right.shape[4]
    half = (XS, ZQ // 2, XS, 2, 2 * nus, mu)
    return pl.pallas_call(
        pairs_kernel,
        grid_spec=pltpu.PrefetchScalarGridSpec(
            num_scalar_prefetch=1,
            grid=(1,),
            in_specs=[pl.BlockSpec((2, 1, mu, orbitals), lambda n, place: (0, place[1], 0, 0))]
            + [pl.BlockSpec(memory_space=pltpu.VMEM)] * XS,
            out_specs=pl.BlockSpec(memory_space=pl.ANY),
            scratch_shapes=[pltpu.VMEM((2, *half), jnp.bfloat16), pltpu.SemaphoreType.DMA((2,))],
        ),
        out_shape=jax.ShapeDtypeStruct((XS, ZH, *half[1:]), jnp.bfloat16),
        compiler_params=VMEM,
        cost_estimate=pl.CostEstimate(
            flops=16 * XS * XS * ZQ * nus * mu * orbitals, bytes_accessed=3 << 20, transcendentals=0
        ),
        name="pairs",
    )(place, *lefts, right)


def dft4(values, sign):
    (r0, i0), (r1, i1), (r2, i2), (r3, i3) = values
    ar, ai, br, bi = r0 + r2, i0 + i2, r0 - r2, i0 - i2
    cr, ci, dr, di = r1 + r3, i1 + i3, r1 - r3, i1 - i3
    if sign < 0:
        return [(ar + cr, ai + ci), (br + di, bi - dr), (ar - cr, ai - ci), (br - di, bi + dr)]
    return [(ar + cr, ai + ci), (br - di, bi + dr), (ar - cr, ai - ci), (br + di, bi - dr)]


def dft16(values, sign):
    out = list(values)
    for slow in range(4):
        out[4 * slow : 4 * slow + 4] = dft4(out[4 * slow : 4 * slow + 4], sign)
    for fast in range(4):
        out[fast::4] = dft4(out[fast::4], sign)
    return out


def spectral_kernel(x_ref, c_ref, out_ref, work_ref, done_ref, sems):
    rows = work_ref.shape[2]
    copies = []
    for n in range(done_ref.shape[0]):
        at = slice(n * rows, (n + 1) * rows)
        for top in range(4):
            values = [
                tuple(x_ref[16 * top + low, part, at].astype(jnp.float32) for part in range(2)) for low in range(16)
            ]
            for low, (re, im) in enumerate(dft16(values, -1)):
                work_ref[0, 16 * top + low] = re
                work_ref[1, 16 * top + low] = im
        for low in range(16):
            values = [(work_ref[0, 16 * top + low], work_ref[1, 16 * top + low]) for top in range(4)]
            weighted = []
            for top, (re, im) in enumerate(dft4(values, -1)):
                c = c_ref[16 * top + low, at].astype(jnp.float32)
                weighted.append(tuple((c * part).astype(jnp.bfloat16).astype(jnp.float32) for part in (re, im)))
            for top, (re, im) in enumerate(dft4(weighted, 1)):
                work_ref[0, 16 * top + low] = re
                work_ref[1, 16 * top + low] = im
        for top in range(4):
            values = [(work_ref[0, 16 * top + low], work_ref[1, 16 * top + low]) for low in range(16)]
            for low, parts in enumerate(dft16(values, 1)):
                for part in range(2):
                    done_ref[n, 16 * top + low, part] = (parts[part] * (1.0 / 64.0)).astype(jnp.bfloat16)
        copies.append(pltpu.make_async_copy(done_ref.at[n], out_ref.at[:, :, pl.ds(n * rows, rows)], sems.at[n]))
        copies[-1].start()
    for copy in copies:
        copy.wait()


def spectral(x, coulomb):
    count, _, nus, mu = x.shape
    rows = 16
    return pl.pallas_call(
        spectral_kernel,
        in_specs=[pl.BlockSpec(memory_space=pltpu.VMEM)] * 2,
        out_specs=pl.BlockSpec(memory_space=pl.ANY),
        out_shape=jax.ShapeDtypeStruct(x.shape, jnp.bfloat16),
        scratch_shapes=[
            pltpu.VMEM((2, count, rows, mu), jnp.float32),
            pltpu.VMEM((nus // rows, count, 2, rows, mu), jnp.bfloat16),
            pltpu.SemaphoreType.DMA((nus // rows,)),
        ],
        compiler_params=VMEM,
        cost_estimate=pl.CostEstimate(flops=32 * count * nus * mu, bytes_accessed=5 << 19, transcendentals=0),
        name="spectral",
    )(x, coulomb)


def apply_kernel(plan, place_ref, kernel_ref, *refs):
    out_ref, blocks_ref, right_ref, done_ref, in_sems, out_sems = refs[-6:]
    mu, orbitals = out_ref.shape[2:]
    tn = (((0,), (0,)), ((), ()))
    gets, puts = [], []
    n = 0
    for d, pieces in enumerate(plan):
        k = (place_ref[1] + XS - d) % XS
        gets.append([pltpu.make_async_copy(kernel_ref.at[:, :, :, k], blocks_ref.at[d], in_sems.at[n])])
        n += 1
        at = 0
        for array, begin, length in pieces:
            source = refs[array].at[pl.ds(begin, length)]
            gets[d].append(pltpu.make_async_copy(source, right_ref.at[d, pl.ds(at, length)], in_sems.at[n]))
            at += length
            n += 1
        puts.append(pltpu.make_async_copy(done_ref.at[d], out_ref.at[:, k], out_sems.at[d]))
    for copy in gets[0] + gets[1]:
        copy.start()
    for d in range(XS):
        for copy in gets[d + 2] if d + 2 < XS else []:
            copy.start()
        for copy in gets[d]:
            copy.wait()
        total = None
        for side in range(2):
            at = (place_ref[0] + side) % ZH
            k_re = blocks_ref[d, :, at, :, 0].reshape(-1, mu)
            k_im = blocks_ref[d, :, at, :, 1].reshape(-1, mu)
            b_re = right_ref[d, :, :, 0, side].reshape(-1, orbitals)
            b_im = right_ref[d, :, :, 1, side].reshape(-1, orbitals)
            first = jnp.concatenate([k_re, k_im], 1)
            second = jnp.concatenate([-k_im, k_re], 1)
            term = lax.dot_general(first, b_re, tn, preferred_element_type=jnp.float32) + lax.dot_general(
                second, b_im, tn, preferred_element_type=jnp.float32
            )
            total = term if total is None else total + term
        done_ref[d, 0] = total[:mu]
        done_ref[d, 1] = total[mu:]
        puts[d].start()
    for copy in puts:
        copy.wait()


def apply(place, kernel, arrays, plan):
    xs, zhs, pairs, kl, _, rows, mu = kernel.shape
    orbitals = arrays[0].shape[-1]
    return pl.pallas_call(
        functools.partial(apply_kernel, plan),
        grid_spec=pltpu.PrefetchScalarGridSpec(
            num_scalar_prefetch=1,
            grid=(1,),
            in_specs=[pl.BlockSpec(memory_space=pl.ANY)] * (1 + len(arrays)),
            out_specs=pl.BlockSpec(memory_space=pl.ANY),
            scratch_shapes=[
                pltpu.VMEM((XS, xs, zhs, pairs, 2, rows, mu), jnp.bfloat16),
                pltpu.VMEM((XS, XS, *arrays[0].shape[1:]), jnp.bfloat16),
                pltpu.VMEM((XS, 2, mu, orbitals), jnp.float32),
                pltpu.SemaphoreType.DMA((XS + sum(map(len, plan)),)),
                pltpu.SemaphoreType.DMA((XS,)),
            ],
        ),
        out_shape=jax.ShapeDtypeStruct((2, kl, mu, orbitals), jnp.float32),
        compiler_params=VMEM,
        cost_estimate=pl.CostEstimate(
            flops=8 * kl * xs * zhs * pairs * rows * mu * orbitals, bytes_accessed=7 << 20, transcendentals=0
        ),
        name="apply",
    )(place, kernel, *arrays)


def swap(blocks, axes):
    return lax.all_to_all(blocks, axes, split_axis=0, concat_axis=0, tiled=True)


def shift(block, d):
    return lax.ppermute(block, "x", [(i, (i + d) % XS) for i in range(XS)])


def on_device(left, right, coulomb):
    parts, kl, nus, orbitals = right.shape
    mu = left.shape[2]
    x = lax.axis_index("x")
    place = jnp.stack([lax.axis_index("zh"), x]).astype(jnp.int32)
    other = lax.ppermute(right, "zh", [(0, 1), (1, 0)])
    sides = make_send(other, 1, make_send(right, 0))
    mine = swap(sides.reshape(kl * ZQ, parts, 2, nus, orbitals), ("x", "zq"))
    mine = mine.reshape(XS, ZQ, parts, 2, nus, orbitals)
    lefts = [left]
    for d in range(1, XS):
        block = lax.dynamic_slice_in_dim(left, (x + d) % XS, 1, 1)
        lefts.append(shift(block, d))
    pairs = make_pairs(place, lefts, mine)
    columns = swap(pairs.reshape(KG * XS, parts, 2 * nus, mu), ("kg", "x"))
    low, high = mine[: XS // 2], mine[XS // 2 :]
    spatial = spectral(columns, coulomb)
    spatial, up, down = lax.optimization_barrier((spatial, shift(low, 1), shift(high, XS - 1)))
    late = jnp.concatenate([shift(high, 1), shift(up, 1), shift(down, XS - 1), shift(low, XS - 1)])
    early = jnp.concatenate([up, down])
    half = XS // 2
    plan = [
        [(0, 0, XS)],
        [(1, 0, half), (2, 0, half)],
        [(2, half, XS)],
        [(2, half + XS, half), (1, half, half)],
    ]
    kernel = swap(spatial.reshape(KG, KL, parts, 2 * nus, mu), "kg")
    return apply(place, kernel.reshape(XS, ZH, ZQ // 2, KL, parts, 2 * nus, mu), [mine, early, late], plan)


def solution(mesh):
    split = Mesh(mesh.devices.reshape(KG, XS, ZH, ZQ), ("kg", "x", "zh", "zq"))
    points = ("x", "zh", "zq")
    in_specs = (P(None, "kg", points, None), P(None, "kg", points, None), P(None, "kg", points))
    out_specs = P(None, "kg", points, None)
    return jax.shard_map(on_device, mesh=split, in_specs=in_specs, out_specs=out_specs, check_vma=False)
```

```python
import functools

import jax
import jax.numpy as jnp
from jax import lax
from jax.experimental import pallas as pl
from jax.experimental.pallas import tpu as pltpu
from jax.sharding import Mesh, PartitionSpec as P

XS, ZH, ZQ = 4, 2, 4
KG, KL = 16, 4
VMEM = pltpu.CompilerParams(vmem_limit_bytes=24 << 20)


def send_kernel(right_ref, *refs):
    out_ref = refs[-1]
    for part in range(2):
        block = right_ref[part]
        for zq in range(ZQ):
            out_ref[:, zq, part, 0] = block


def make_send(right, side, base=None):
    parts, kl, nus, orbitals = right.shape
    more = [] if base is None else [base]
    return pl.pallas_call(
        send_kernel,
        grid=(1,),
        in_specs=[pl.BlockSpec(right.shape, lambda n: (0, 0, 0, 0))] + [pl.BlockSpec(memory_space=pl.ANY)] * len(more),
        out_specs=pl.BlockSpec((kl, ZQ, parts, 1, nus, orbitals), lambda n: (0, 0, 0, side, 0, 0)),
        out_shape=jax.ShapeDtypeStruct((kl, ZQ, parts, 2, nus, orbitals), right.dtype),
        input_output_aliases={1: 0} if more else {},
        compiler_params=VMEM,
        cost_estimate=pl.CostEstimate(flops=0, bytes_accessed=5 << 17, transcendentals=0),
        name="send",
    )(right, *more)


def pairs_kernel(place_ref, *refs):
    lefts, (right_ref, out_ref, done_ref, sems) = refs[:XS], refs[XS:]
    mu, orbitals = lefts[0].shape[2:]
    nt = (((1,), (1,)), ((), ()))
    shape = (XS, ZQ // 2, done_ref.shape[5], mu)
    copies = []
    for side in range(2):
        b_re = right_ref[:, :, 0, side].reshape(-1, orbitals)
        b_im = right_ref[:, :, 1, side].reshape(-1, orbitals)
        for d, left_ref in enumerate(lefts):
            a_re, a_im = left_ref[0, 0], left_ref[1, 0]
            first = jnp.concatenate([a_re, a_im], 0)
            second = jnp.concatenate([a_im, -a_re], 0)
            both = lax.dot_general(b_re, first, nt, preferred_element_type=jnp.float32) + lax.dot_general(
                b_im, second, nt, preferred_element_type=jnp.float32
            )
            both = both.astype(jnp.bfloat16)
            at = (place_ref[1] + XS - d) % XS
            done_ref[side, :, :, at, 0] = both[:, :mu].reshape(shape)
            done_ref[side, :, :, at, 1] = both[:, mu:].reshape(shape)
        copies.append(
            pltpu.make_async_copy(done_ref.at[side], out_ref.at[:, (place_ref[0] + side) % ZH], sems.at[side])
        )
        copies[-1].start()
    for copy in copies:
        copy.wait()


def make_pairs(place, lefts, right):
    _, _, mu, orbitals = lefts[0].shape
    nus = right.shape[4]
    half = (XS, ZQ // 2, XS, 2, 2 * nus, mu)
    return pl.pallas_call(
        pairs_kernel,
        grid_spec=pltpu.PrefetchScalarGridSpec(
            num_scalar_prefetch=1,
            grid=(1,),
            in_specs=[pl.BlockSpec((2, 1, mu, orbitals), lambda n, place: (0, place[1], 0, 0))]
            + [pl.BlockSpec(memory_space=pltpu.VMEM)] * XS,
            out_specs=pl.BlockSpec(memory_space=pl.ANY),
            scratch_shapes=[pltpu.VMEM((2, *half), jnp.bfloat16), pltpu.SemaphoreType.DMA((2,))],
        ),
        out_shape=jax.ShapeDtypeStruct((XS, ZH, *half[1:]), jnp.bfloat16),
        compiler_params=VMEM,
        cost_estimate=pl.CostEstimate(
            flops=16 * XS * XS * ZQ * nus * mu * orbitals, bytes_accessed=3 << 20, transcendentals=0
        ),
        name="pairs",
    )(place, *lefts, right)


def dft4(values, sign):
    (r0, i0), (r1, i1), (r2, i2), (r3, i3) = values
    ar, ai, br, bi = r0 + r2, i0 + i2, r0 - r2, i0 - i2
    cr, ci, dr, di = r1 + r3, i1 + i3, r1 - r3, i1 - i3
    if sign < 0:
        return [(ar + cr, ai + ci), (br + di, bi - dr), (ar - cr, ai - ci), (br - di, bi + dr)]
    return [(ar + cr, ai + ci), (br - di, bi + dr), (ar - cr, ai - ci), (br + di, bi - dr)]


def dft16(values, sign):
    out = list(values)
    for slow in range(4):
        out[4 * slow : 4 * slow + 4] = dft4(out[4 * slow : 4 * slow + 4], sign)
    for fast in range(4):
        out[fast::4] = dft4(out[fast::4], sign)
    return out


def spectral_kernel(x_ref, c_ref, out_ref, work_ref, done_ref, sems):
    rows = work_ref.shape[2]
    copies = []
    for n in range(done_ref.shape[0]):
        at = slice(n * rows, (n + 1) * rows)
        for top in range(4):
            values = [
                tuple(x_ref[16 * top + low, part, at].astype(jnp.float32) for part in range(2)) for low in range(16)
            ]
            for low, (re, im) in enumerate(dft16(values, -1)):
                work_ref[0, 16 * top + low] = re
                work_ref[1, 16 * top + low] = im
        for low in range(16):
            values = [(work_ref[0, 16 * top + low], work_ref[1, 16 * top + low]) for top in range(4)]
            weighted = []
            for top, (re, im) in enumerate(dft4(values, -1)):
                c = c_ref[16 * top + low, at].astype(jnp.float32)
                weighted.append(tuple((c * part).astype(jnp.bfloat16).astype(jnp.float32) for part in (re, im)))
            for top, (re, im) in enumerate(dft4(weighted, 1)):
                work_ref[0, 16 * top + low] = re
                work_ref[1, 16 * top + low] = im
        for top in range(4):
            values = [(work_ref[0, 16 * top + low], work_ref[1, 16 * top + low]) for low in range(16)]
            for low, parts in enumerate(dft16(values, 1)):
                for part in range(2):
                    done_ref[n, 16 * top + low, part] = (parts[part] * (1.0 / 64.0)).astype(jnp.bfloat16)
        copies.append(pltpu.make_async_copy(done_ref.at[n], out_ref.at[:, :, pl.ds(n * rows, rows)], sems.at[n]))
        copies[-1].start()
    for copy in copies:
        copy.wait()


def spectral(x, coulomb):
    count, _, nus, mu = x.shape
    rows = 16
    return pl.pallas_call(
        spectral_kernel,
        in_specs=[pl.BlockSpec(memory_space=pltpu.VMEM)] * 2,
        out_specs=pl.BlockSpec(memory_space=pl.ANY),
        out_shape=jax.ShapeDtypeStruct(x.shape, jnp.bfloat16),
        scratch_shapes=[
            pltpu.VMEM((2, count, rows, mu), jnp.float32),
            pltpu.VMEM((nus // rows, count, 2, rows, mu), jnp.bfloat16),
            pltpu.SemaphoreType.DMA((nus // rows,)),
        ],
        compiler_params=VMEM,
        cost_estimate=pl.CostEstimate(flops=32 * count * nus * mu, bytes_accessed=5 << 19, transcendentals=0),
        name="spectral",
    )(x, coulomb)


def apply_kernel(plan, place_ref, kernel_ref, *refs):
    out_ref, blocks_ref, right_ref, done_ref, in_sems, out_sems = refs[-6:]
    mu, orbitals = out_ref.shape[2:]
    tn = (((0,), (0,)), ((), ()))
    gets, puts = [], []
    n = 0
    for d, pieces in enumerate(plan):
        k = (place_ref[1] + XS - d) % XS
        gets.append([pltpu.make_async_copy(kernel_ref.at[:, :, :, k], blocks_ref.at[d], in_sems.at[n])])
        n += 1
        at = 0
        for array, begin, length in pieces:
            source = refs[array].at[pl.ds(begin, length)]
            gets[d].append(pltpu.make_async_copy(source, right_ref.at[d, pl.ds(at, length)], in_sems.at[n]))
            at += length
            n += 1
        puts.append(pltpu.make_async_copy(done_ref.at[d], out_ref.at[:, k], out_sems.at[d]))
    for copy in gets[0] + gets[1]:
        copy.start()
    for d in range(XS):
        for copy in gets[d + 2] if d + 2 < XS else []:
            copy.start()
        for copy in gets[d]:
            copy.wait()
        total = None
        for side in range(2):
            at = (place_ref[0] + side) % ZH
            k_re = blocks_ref[d, :, at, :, 0].reshape(-1, mu)
            k_im = blocks_ref[d, :, at, :, 1].reshape(-1, mu)
            b_re = right_ref[d, :, :, 0, side].reshape(-1, orbitals)
            b_im = right_ref[d, :, :, 1, side].reshape(-1, orbitals)
            first = jnp.concatenate([k_re, k_im], 1)
            second = jnp.concatenate([-k_im, k_re], 1)
            term = lax.dot_general(first, b_re, tn, preferred_element_type=jnp.float32) + lax.dot_general(
                second, b_im, tn, preferred_element_type=jnp.float32
            )
            total = term if total is None else total + term
        done_ref[d, 0] = total[:mu]
        done_ref[d, 1] = total[mu:]
        puts[d].start()
    for copy in puts:
        copy.wait()


def apply(place, kernel, arrays, plan):
    xs, zhs, pairs, kl, _, rows, mu = kernel.shape
    orbitals = arrays[0].shape[-1]
    return pl.pallas_call(
        functools.partial(apply_kernel, plan),
        grid_spec=pltpu.PrefetchScalarGridSpec(
            num_scalar_prefetch=1,
            grid=(1,),
            in_specs=[pl.BlockSpec(memory_space=pl.ANY)] * 2
            + [pl.BlockSpec(memory_space=pltpu.HBM)] * (len(arrays) - 1),
            out_specs=pl.BlockSpec(memory_space=pl.ANY),
            scratch_shapes=[
                pltpu.VMEM((XS, xs, zhs, pairs, 2, rows, mu), jnp.bfloat16),
                pltpu.VMEM((XS, XS, *arrays[0].shape[1:]), jnp.bfloat16),
                pltpu.VMEM((XS, 2, mu, orbitals), jnp.float32),
                pltpu.SemaphoreType.DMA((XS + sum(map(len, plan)),)),
                pltpu.SemaphoreType.DMA((XS,)),
            ],
        ),
        out_shape=jax.ShapeDtypeStruct((2, kl, mu, orbitals), jnp.float32),
        compiler_params=VMEM,
        cost_estimate=pl.CostEstimate(
            flops=8 * kl * xs * zhs * pairs * rows * mu * orbitals, bytes_accessed=7 << 20, transcendentals=0
        ),
        name="apply",
    )(place, kernel, *arrays)


def swap(blocks, axes):
    return lax.all_to_all(blocks, axes, split_axis=0, concat_axis=0, tiled=True)


def shift(block, d):
    return lax.ppermute(block, "x", [(i, (i + d) % XS) for i in range(XS)])


def on_device(left, right, coulomb):
    parts, kl, nus, orbitals = right.shape
    mu = left.shape[2]
    x = lax.axis_index("x")
    place = jnp.stack([lax.axis_index("zh"), x]).astype(jnp.int32)
    other = lax.ppermute(right, "zh", [(0, 1), (1, 0)])
    sides = make_send(other, 1, make_send(right, 0))
    mine = swap(sides.reshape(kl * ZQ, parts, 2, nus, orbitals), ("x", "zq"))
    mine = mine.reshape(XS, ZQ, parts, 2, nus, orbitals)
    lefts = [left]
    for d in range(1, XS):
        block = lax.dynamic_slice_in_dim(left, (x + d) % XS, 1, 1)
        lefts.append(shift(block, d))
    pairs = make_pairs(place, lefts, mine)
    columns = swap(pairs.reshape(KG * XS, parts, 2 * nus, mu), ("kg", "x"))
    low, high = mine[: XS // 2], mine[XS // 2 :]
    spatial = spectral(columns, coulomb)
    spatial, up, down = lax.optimization_barrier((spatial, shift(low, 1), shift(high, XS - 1)))
    late = jnp.concatenate([shift(high, 1), shift(up, 1), shift(down, XS - 1), shift(low, XS - 1)])
    early = jnp.concatenate([up, down])
    half = XS // 2
    plan = [
        [(0, 0, XS)],
        [(1, 0, half), (2, 0, half)],
        [(2, half, XS)],
        [(2, half + XS, half), (1, half, half)],
    ]
    kernel = swap(spatial.reshape(KG, KL, parts, 2 * nus, mu), "kg")
    return apply(place, kernel.reshape(XS, ZH, ZQ // 2, KL, parts, 2 * nus, mu), [mine, early, late], plan)


def solution(mesh):
    split = Mesh(mesh.devices.reshape(KG, XS, ZH, ZQ), ("kg", "x", "zh", "zq"))
    points = ("x", "zh", "zq")
    in_specs = (P(None, "kg", points, None), P(None, "kg", points, None), P(None, "kg", points))
    out_specs = P(None, "kg", points, None)
    return jax.shard_map(on_device, mesh=split, in_specs=in_specs, out_specs=out_specs, check_vma=False)
```
